128 devices in a mesh: dp: 8 (over y, core), tm: 16 (over z, x).
Axes of the slice: x: 4, y: 4, z: 4, core: 2. Of those that a mesh axis runs over, the one named last changes fastest.
Arguments:
- signal: bfloat16 [8, 256, 32768], P('dp', None, 'tm'), may hold values from -6 to 6
- lengths: int32 [8, 5], P('dp'), may hold values from 1 to 256, 512 in all within a row
- conv_dilated: bfloat16 [2, 256, 1792], replicated, may hold values from -0.125 to 0.125
- conv_point: bfloat16 [2, 256, 256], replicated, may hold values from -0.375 to 0.375
- conv_down: bfloat16 [16, 512, 256], replicated, may hold values from -0.09375 to 0.09375
- snake_alpha: float32 [5, 256], replicated, may hold values from 0.3 to 3
- out_grad: bfloat16 [8, 512, 4096], P('dp', None, 'tm'), may hold values from -6 to 6
Outputs:
- block_output: bfloat16 [8, 512, 4096], P('dp', None, 'tm')
- signal_grad: bfloat16 [8, 256, 32768], P('dp', None, 'tm')
- grad_dilated: float32 [2, 256, 1792], replicated
- grad_point: float32 [2, 256, 256], replicated
- grad_down: float32 [16, 512, 256], replicated
- grad_alpha: float32 [5, 256], replicated
The draws below stay inside these ranges and needn't reach their ends.
Inputs may be any that keep to these rules, and one draw needn't show every extreme that they name: Each row packs 4 recordings end to end from the group's first sample, their lengths in tiles of 64 samples, followed by the number of unused tiles at the group's end; a row sums to 512 and its largest entry is exactly 256.
All inputs are finite; a program needn't handle non-finite values.
Results may differ from the reference program's by a relative error of at most 0.038.
The reference program's roundings to bfloat16 on the way count: a program that leaves them out, or rounds other values in their place, can miss the bound.
Values may be sent and summed in bfloat16 or wider, within the bound.
A program may use at most 192 MiB of HBM per device.

```python
import math
import jax
import jax.numpy as jnp
import numpy as np
from jax import lax

C = 256
FILTER_TAPS = 7
STRIDE = 8
FIRST_DILATION = 3
SECOND_DILATION = 9
TILE = 64
REC = 4
GROUPS = 8
TIME = 32768
TILES = 512
MOST = 256
ROWS = 4096


def levels(stream_key, dims, split, least, largest):
    level, own = 1.0, jax.random.fold_in(stream_key, 6)
    for position, shards_of in split:
        steps = jnp.exp(jax.random.uniform(jax.random.fold_in(own, position), (shards_of,), jnp.float32, least / len(split), largest / len(split)))
        level = level * jnp.repeat(steps, dims[position] // shards_of).reshape([-1 if axis == position else 1 for axis in range(len(dims))])
    return level


def split_up(number_of, total, most, lean):
    portions = [(1 << 20) // math.isqrt(rank ** lean) + 1 for rank in range(2, number_of + 1)]
    spare, counts = total - most - (number_of - 1), [1] * (number_of - 1)
    while spare > 0:
        movable = [i for i in range(number_of - 1) if counts[i] < most]
        whole, remaining = sum([portions[i] for i in movable]), spare
        for i in movable:
            addition = min(most - counts[i], max(1, remaining * portions[i] // whole), spare)
            counts[i] = counts[i] + addition
            spare = spare - addition
    return np.array([most] + counts)


def ragged_sizes(key, count, total, most, lean):
    if count == 2:
        one = jax.random.randint(key, (), max(1, total - most), min(most, total - 1) + 1)
        return jnp.stack([one, total - one])
    sizes = jnp.asarray(split_up(count, total, most, lean), jnp.int32)
    pairs = (count - 1) // 2
    source_of, taker = sizes[1:1 + 2 * pairs:2], sizes[2:2 + 2 * pairs:2]
    slack = jnp.minimum(source_of - 1, most - taker)
    shifted = jax.random.randint(jax.random.fold_in(key, 1), (pairs,), 0, 1 << 20) % (slack + 1)
    sizes = sizes.at[1:1 + 2 * pairs:2].set(source_of - shifted).at[2:2 + 2 * pairs:2].set(taker + shifted)
    return sizes[jax.random.permutation(jax.random.fold_in(key, 2), count)]


def noise(own_key, shape, deviation, bound, cuts=(), kind=jnp.bfloat16):
    values = jax.random.normal(own_key, shape, jnp.float32) * deviation
    if len(cuts) > 0:
        values = levels(own_key, shape, cuts, -0.22, 0.18) * values
    return jnp.clip(values, min=-bound, max=bound).astype(kind)


def setup_inputs(seed: int = 0) -> dict:
    seeds = jax.random.split(jax.random.key(seed), 8)
    signal = noise(seeds[0], (GROUPS, C, TIME), 1.0, 6.0, ((0, 8), (2, 16)))
    lengths = jax.vmap(lambda own: ragged_sizes(own, REC + 1, TILES, MOST, 2))(jax.random.split(seeds[1], GROUPS)).reshape((GROUPS, REC + 1)).astype(jnp.int32)
    conv_dilated = noise(seeds[2], (2, C, FILTER_TAPS * C), (FILTER_TAPS * C) ** -0.5, 0.125)
    conv_point = noise(seeds[3], (2, C, C), C ** -0.5, 0.375)
    conv_down = noise(seeds[4], (2 * STRIDE, 2 * C, C), (2 * STRIDE * C) ** -0.5, 0.09375)
    snake_alpha = jnp.clip(jnp.exp(jax.random.uniform(seeds[5], (5, C), jnp.float32, math.log(0.3), math.log(3.0))), 0.3, 3.0)
    out_grad = noise(seeds[6], (GROUPS, 2 * C, ROWS), 1.0, 6.0, ((0, 8), (2, 16)))
    return {"signal": signal, "lengths": lengths, "conv_dilated": conv_dilated, "conv_point": conv_point, "conv_down": conv_down, "snake_alpha": snake_alpha, "out_grad": out_grad}


def snake_value(values, alpha_col):
    return values + jnp.sin(alpha_col * values) ** 2 / alpha_col


def snake_slope(values, alpha_col):
    return 1.0 + jnp.sin(2.0 * alpha_col * values)


def snake_alpha_term(values, alpha_col):
    return values * jnp.sin(2.0 * alpha_col * values) / alpha_col - jnp.sin(alpha_col * values) ** 2 / (alpha_col * alpha_col)


def segment_ids(bounds, first_pos, extent, overall):
    places = first_pos + jnp.arange(extent, dtype=jnp.int32)
    record = jnp.sum((places[:, None] >= bounds[None, :]).astype(jnp.int32), axis=1, dtype=jnp.int32)
    inside = (places >= 0) & (places < overall) & (record < REC)
    return jnp.where(inside, record, -places - 1000000)


def unit_forward(unit_in, labels, dilated, point_weight, alpha_a, alpha_b, dilation):
    radius = (FILTER_TAPS // 2) * dilation
    signal_length = unit_in.shape[1] - 2 * radius
    activated = snake_value(unit_in.astype(jnp.float32), alpha_a).astype(jnp.bfloat16)
    centre = labels[radius:radius + signal_length]
    pieces = []
    for tap_no in range(FILTER_TAPS):
        kept_mask = (labels[tap_no * dilation:tap_no * dilation + signal_length] == centre).astype(jnp.bfloat16)
        pieces.append(activated[:, tap_no * dilation:tap_no * dilation + signal_length] * kept_mask[None, :])
    columns = jnp.concatenate(pieces, axis=0)
    hidden = jnp.dot(dilated, columns, preferred_element_type=jnp.float32)
    shaped = snake_value(hidden, alpha_b).astype(jnp.bfloat16)
    pointwise = jnp.dot(point_weight, shaped, preferred_element_type=jnp.float32)
    unit_out = (unit_in[:, radius:radius + signal_length].astype(jnp.float32) + pointwise).astype(jnp.bfloat16)
    return unit_out, (columns, hidden, shaped)


def unit_backward(grad_out, grad_anchor, in_anchor, unit_in, stored, dilated, point_weight, alpha_a, alpha_b, dilation, labels_at, samples):
    columns, hidden, shaped = stored
    radius = (FILTER_TAPS // 2) * dilation
    out_anchor = in_anchor + radius
    extent = grad_out.shape[1]
    offset = grad_anchor - out_anchor
    own_grad = -grad_anchor
    own_out = -out_anchor
    back_point = lax.dot_general(point_weight, grad_out, (((0,), (0,)), ((), ())), preferred_element_type=jnp.float32)
    hidden_part = hidden[:, offset:offset + extent]
    grad_hidden = (back_point * snake_slope(hidden_part, alpha_b)).astype(jnp.bfloat16)
    term_b = jnp.sum(back_point[:, own_grad:own_grad + samples] * snake_alpha_term(hidden_part[:, own_grad:own_grad + samples], alpha_b), axis=1)
    grad_point = lax.dot_general(grad_out[:, own_grad:own_grad + samples], shaped[:, own_out:own_out + samples], (((1,), (1,)), ((), ())), preferred_element_type=jnp.float32)
    grad_dilated = lax.dot_general(grad_hidden[:, own_grad:own_grad + samples], columns[:, own_out:own_out + samples], (((1,), (1,)), ((), ())), preferred_element_type=jnp.float32)
    wide_len = extent
    labels = labels_at(grad_anchor - radius, wide_len + 2 * radius)
    centre = labels[radius:radius + wide_len]
    tap_masks = jnp.stack([labels[tap_no * dilation:tap_no * dilation + wide_len] == centre for tap_no in range(FILTER_TAPS)]).astype(jnp.float32)
    channels = grad_hidden.shape[0]
    spread = lax.dot_general(dilated, grad_hidden, (((0,), (0,)), ((), ())), preferred_element_type=jnp.float32).reshape(FILTER_TAPS, channels, wide_len) * tap_masks[:, None, :]
    signal_length = wide_len - 2 * radius
    grad_act = sum(spread[tap_no, :, (FILTER_TAPS - 1 - tap_no) * dilation:(FILTER_TAPS - 1 - tap_no) * dilation + signal_length] for tap_no in range(FILTER_TAPS))
    act_anchor = grad_anchor + radius
    unit_part = unit_in[:, act_anchor - in_anchor:act_anchor - in_anchor + signal_length].astype(jnp.float32)
    grad_in = (grad_out[:, radius:radius + signal_length].astype(jnp.float32) + grad_act * snake_slope(unit_part, alpha_a)).astype(jnp.bfloat16)
    own_act = -act_anchor
    term_a = jnp.sum(grad_act[:, own_act:own_act + samples] * snake_alpha_term(unit_part[:, own_act:own_act + samples], alpha_a), axis=1)
    return grad_in, act_anchor, (grad_dilated, grad_point, term_a, term_b)


def down_forward(down_in, in_anchor, alpha_col, conv_down, labels_at, samples):
    half_step = STRIDE // 2
    blocks = samples // STRIDE
    offset = -half_step - in_anchor
    window = down_in[:, offset:offset + samples + STRIDE].astype(jnp.float32)
    activated = snake_value(window, alpha_col).astype(jnp.bfloat16)
    channels = activated.shape[0]
    folded = activated.reshape(channels, blocks + 1, STRIDE).transpose(2, 0, 1)
    columns = jnp.concatenate([folded[:, :, :blocks], folded[:, :, 1:]], axis=0)
    labels = labels_at(-half_step, samples + STRIDE).reshape(blocks + 1, STRIDE).T
    tap_ids = jnp.concatenate([labels[:, :blocks], labels[:, 1:]], axis=0)
    kept_mask = (tap_ids == labels[half_step, :blocks][None, :]).astype(jnp.bfloat16)
    columns = columns * kept_mask[:, None, :]
    produced = lax.dot_general(conv_down.astype(jnp.float32), columns.astype(jnp.float32), (((0, 2), (0, 1)), ((), ())), precision=lax.Precision.HIGHEST)
    return produced, columns


def down_backward(grad_rows, margin, columns, conv_down, labels_at, samples):
    half_step = STRIDE // 2
    blocks = samples // STRIDE
    extent = blocks + 2 * margin
    spread = lax.dot_general(conv_down.astype(jnp.float32), grad_rows.astype(jnp.float32), (((1,), (0,)), ((), ())), precision=lax.Precision.HIGHEST)
    first_pos = -STRIDE * margin - half_step
    labels = labels_at(first_pos, STRIDE * (extent + 1)).reshape(extent + 1, STRIDE).T
    tap_ids = jnp.concatenate([labels[:, :extent], labels[:, 1:]], axis=0)
    kept_mask = (tap_ids == labels[half_step, :extent][None, :]).astype(jnp.float32)
    spread = spread * kept_mask[:, None, :]
    channels = spread.shape[1]
    padding = jnp.zeros((STRIDE, channels, 1), jnp.float32)
    placed = jnp.concatenate([spread[:STRIDE], padding], axis=2) + jnp.concatenate([padding, spread[STRIDE:]], axis=2)
    grad_act = placed.transpose(1, 2, 0).reshape(channels, STRIDE * (extent + 1))
    own_rows = grad_rows[:, margin:margin + blocks]
    grad_down = jnp.einsum("oj,kcj->koc", own_rows.astype(jnp.float32), columns.astype(jnp.float32), precision=lax.Precision.HIGHEST)
    return grad_act, first_pos, grad_down


def group_pass(group_signal, group_lengths, group_grad, conv_dilated, conv_point, conv_down, snake_alpha):
    samples = group_signal.shape[1]
    bounds = jnp.cumsum(group_lengths[:REC], dtype=jnp.int32) * TILE

    def labels_at(anchor, extent):
        return segment_ids(bounds, anchor, extent, samples)

    alphas = snake_alpha[:, :, None]
    live_mask = (labels_at(0, samples) >= 0).astype(jnp.bfloat16)
    source = group_signal * live_mask[None, :]
    dilation_list = (FIRST_DILATION, SECOND_DILATION)
    total_radius = (FILTER_TAPS // 2) * (FIRST_DILATION + SECOND_DILATION)
    running_offset = jnp.pad(source, ((0, 0), (2 * total_radius, 2 * total_radius)))
    current_start = -2 * total_radius
    unit_inputs = []
    unit_offsets = []
    unit_saves = []
    for unit_index in range(2):
        unit_inputs.append(running_offset)
        unit_offsets.append(current_start)
        running_offset, stored = unit_forward(running_offset, labels_at(current_start, running_offset.shape[1]), conv_dilated[unit_index], conv_point[unit_index], alphas[2 * unit_index], alphas[2 * unit_index + 1], dilation_list[unit_index])
        unit_saves.append(stored)
        current_start = current_start + (FILTER_TAPS // 2) * dilation_list[unit_index]
    block_out = running_offset
    block_start = current_start
    produced, down_columns = down_forward(block_out, block_start, alphas[4], conv_down, labels_at, samples)
    margin = (total_radius + 2 * STRIDE - 1 - STRIDE // 2) // STRIDE
    grad_rows = jnp.pad(group_grad, ((0, 0), (margin, margin)))
    grad_act, act_start, grad_down = down_backward(grad_rows, margin, down_columns, conv_down, labels_at, samples)
    offset = block_start - act_start
    block_value = block_out.astype(jnp.float32)
    grad_flow = grad_act[:, offset:offset + block_out.shape[1]]
    grad_current = (grad_flow * snake_slope(block_value, alphas[4])).astype(jnp.bfloat16)
    own_block = -block_start
    term_down = jnp.sum(grad_flow[:, own_block:own_block + samples] * snake_alpha_term(block_value[:, own_block:own_block + samples], alphas[4]), axis=1)
    grad_start = block_start
    unit_grads = [None, None]
    for unit_index in (1, 0):
        grad_current, grad_start, pieces = unit_backward(grad_current, grad_start, unit_offsets[unit_index], unit_inputs[unit_index], unit_saves[unit_index], conv_dilated[unit_index], conv_point[unit_index], alphas[2 * unit_index], alphas[2 * unit_index + 1], dilation_list[unit_index], labels_at, samples)
        unit_grads[unit_index] = pieces
    signal_grad = grad_current * live_mask[None, :]
    grad_dilated = jnp.stack([unit_grads[0][0], unit_grads[1][0]])
    grad_point = jnp.stack([unit_grads[0][1], unit_grads[1][1]])
    grad_alpha = jnp.stack([unit_grads[0][2], unit_grads[0][3], unit_grads[1][2], unit_grads[1][3], term_down])
    return (produced.astype(jnp.bfloat16), signal_grad, grad_dilated, grad_point, grad_down, grad_alpha)


def reference(signal, lengths, conv_dilated, conv_point, conv_down, snake_alpha, out_grad):
    def one_group(group_items):
        return group_pass(group_items[0], group_items[1], group_items[2], conv_dilated, conv_point, conv_down, snake_alpha)

    results = lax.map(one_group, (signal, lengths, out_grad))
    return (results[0], results[1], jnp.sum(results[2], axis=0), jnp.sum(results[3], axis=0), jnp.sum(results[4], axis=0), jnp.sum(results[5], axis=0))
```

```python
import functools

import jax
import jax.numpy as jnp
from jax import lax
from jax.experimental import pallas as pl
from jax.experimental.pallas import tpu as pltpu
from jax.sharding import PartitionSpec as P

TAPS = 7
STRIDE = 8
DILATIONS = (3, 9)
TILE = 64
REC = 4
C = 256
HALO = 128
GHALO = HALO // STRIDE
BLOCK = 256
F32 = jnp.float32
BF16 = jnp.bfloat16

SIN_PI = (3.14159258, -5.16770688, 2.55003138, -0.59804517, 0.07722012)
COS_PI = (0.99999995, -4.93479286, 4.05841191, -1.33188013, 0.21969673)


def dot(a, b):
    return jnp.dot(a, b, preferred_element_type=F32)


def dot_nt(a, b):
    return lax.dot_general(a, b, (((1,), (1,)), ((), ())), preferred_element_type=F32)


def poly(coefs, x):
    total = coefs[-1]
    for c in coefs[-2::-1]:
        total = total * x + c
    return total


def sine_parts(turns):
    f = turns - jnp.round(turns)
    x = f * f
    s = f * poly(SIN_PI, x)
    c = poly(COS_PI, x)
    sc = s * c
    return sc + sc, s * s


def compute_kernel(samples, len_ref, sig_ref, gext_ref, wd_ref, wp_ref, wdn_ref, al_ref,
                   out_ref, sg_ref, gw_ref, gdn_ref, ga_ref,
                   cols0, cols1, act, u0, u1, b0, b1, grad, slope, sa, tm0, tm1, zcols,
                   gtf, gt, wt, wpt, masks, live, kcol, acc, hbuf, stage, stage_sem):
    cols_of, u_of, b_of = (cols0, cols1), (u0, u1), (b0, b1)
    extent = samples + 2 * HALO
    tiles = extent // 128
    own_tiles = samples // 128
    blocks = extent // BLOCK
    own_blocks = samples // BLOCK
    rows_j = samples // STRIDE
    all_j = extent // STRIDE
    anchor = lax.axis_index("tm") * samples
    overall = samples * lax.axis_size("tm")

    bounds = []
    total = 0
    for r in range(REC):
        total = total + len_ref[0, r]
        bounds.append(total * TILE)

    def label(p):
        rec = jnp.zeros(p.shape, jnp.int32)
        for b in bounds:
            rec = rec + jnp.where(p >= b, 1, 0)
        ok = (p >= 0) & (p < overall) & (rec < REC)
        return jnp.where(ok, rec, -1)

    def mask_body(j, _):
        lanes = lax.broadcasted_iota(jnp.int32, (16, 128), 1) + j * 128
        p = jnp.where(lanes < samples + HALO, lanes, lanes - extent) + anchor
        here = label(p)
        off = pl.ds(pl.multiple_of(j * 128, 128), 128)
        live[:, off] = jnp.where(here >= 0, 1.0, 0.0).astype(BF16)
        slot = 0
        for d in DILATIONS:
            for k in range(TAPS):
                if k != TAPS // 2:
                    there = label(p + (k - TAPS // 2) * d)
                    masks[slot, :, off] = jnp.where(here == there, 1.0, 0.0).astype(BF16)
                    slot += 1
        return 0

    lax.fori_loop(0, tiles, mask_body, 0)

    for i in range(5):
        col = jnp.broadcast_to(al_ref[i : i + 1, :], (128, C)).T
        kcol[0, i] = col * (1.0 / 3.14159265358979)
        kcol[1, i] = 1.0 / col
    acc[...] = jnp.zeros_like(acc)

    def activate(v, i, rows):
        k0 = kcol[0, i, rows, :]
        k1 = kcol[1, i, rows, :]
        s2, sq = sine_parts(v * k0)
        q = sq * k1
        return v + q, s2, (v * s2 - q) * k1

    def first_body(r, _):
        rows = pl.ds(pl.multiple_of(r * 32, 32), 32)
        for j in range(tiles):
            lanes = slice(j * 128, j * 128 + 128)
            lv = live[:, lanes]
            v = sig_ref[rows, lanes] * jnp.concatenate([lv, lv], axis=0)
            u0[rows, lanes] = v
            a, s2, t = activate(v.astype(F32), 0, rows)
            act[rows, lanes] = a.astype(BF16)
            slope[0, rows, lanes] = (1.0 + s2).astype(BF16)
            if j < own_tiles:
                sa[0, rows, lanes] = t.astype(BF16)
        return 0

    lax.fori_loop(0, C // 32, first_body, 0)

    def shift_pass(src, cols, unit):
        d = DILATIONS[unit]

        def body(r, _):
            rows = pl.ds(pl.multiple_of(r * 16, 16), 16)
            x = src[rows, :]
            for k in range(TAPS):
                by = (k - TAPS // 2) * d
                y = x
                if by:
                    y = jnp.concatenate([x[:, by % extent:], x[:, : by % extent]], axis=1)
                    slot = unit * (TAPS - 1) + (k if k < TAPS // 2 else k - 1)
                    y = y * masks[slot]
                cols[pl.ds(pl.multiple_of(r * 16 + k * C, 16), 16), :] = y
            return 0

        lax.fori_loop(0, C // 16, body, 0)

    def over_blocks(fn):
        lax.fori_loop(0, own_blocks, lambda nb, _: (fn(nb, True), 0)[1], 0)
        for nb in range(own_blocks, blocks):
            fn(nb, False)

    def block_lanes(nb, half=None):
        if half is None:
            return pl.ds(pl.multiple_of(nb * BLOCK, BLOCK), BLOCK)
        return pl.ds(pl.multiple_of(nb * BLOCK + half * 128, 128), 128)

    def forward(unit):
        cols, b_ref, u_ref = cols_of[unit], b_of[unit], u_of[unit]
        hi, ui = 2 * unit + 1, 2 * unit + 2

        def fn(nb, own):
            lanes = block_lanes(nb)
            hbuf[...] = dot(wd_ref[unit], cols[:, lanes])
            for r in range(0, C, 32):
                rows = slice(r, r + 32)
                for half in range(2):
                    hl = block_lanes(nb, half)
                    v = hbuf[rows, half * 128 : half * 128 + 128]
                    a, s2, t = activate(v, hi, rows)
                    b_ref[rows, hl] = a.astype(BF16)
                    slope[hi, rows, hl] = (1.0 + s2).astype(BF16)
                    if own:
                        sa[hi, rows, hl] = t.astype(BF16)
            hbuf[...] = dot(wp_ref[unit], b_ref[:, lanes])
            for r in range(0, C, 32):
                rows = slice(r, r + 32)
                for half in range(2):
                    hl = block_lanes(nb, half)
                    u = (u_ref[rows, hl].astype(F32) + hbuf[rows, half * 128 : half * 128 + 128]).astype(BF16)
                    if unit == 0:
                        u1[rows, hl] = u
                    a, s2, t = activate(u.astype(F32), ui, rows)
                    act[rows, hl] = a.astype(BF16)
                    slope[ui, rows, hl] = (1.0 + s2).astype(BF16)
                    if own:
                        sa[ui, rows, hl] = t.astype(BF16)

        over_blocks(fn)

    for unit in range(2):
        shift_pass(act, cols_of[unit], unit)
        forward(unit)

    halves = (tm0, tm1)

    def z_body(j, _):
        src = pl.ds(pl.multiple_of(lax.rem(j + tiles - 1, tiles) * 128, 128), 128)
        dst = pl.ds(pl.multiple_of(j * 128, 128), 128)
        for h in range(2):
            halves[h][dst, :] = act[h * 128 : h * 128 + 128, src].astype(F32).T
        return 0

    lax.fori_loop(0, tiles, z_body, 0)

    def edge_mask(count, first, step):
        j = lax.broadcasted_iota(jnp.int32, (count, 128), 0) + first
        p = j * STRIDE + anchor
        return jnp.where(label(p) == label(p + step), 1.0, 0.0)

    before = edge_mask(rows_j, 0, -1)
    after = edge_mask(rows_j, 0, STRIDE)
    for k in range(2 * STRIDE):
        for h in range(2):
            z = halves[h][pl.ds(HALO - STRIDE // 2 + k, rows_j, stride=STRIDE), :]
            if k < STRIDE // 2:
                z = z * before
            elif k >= STRIDE // 2 + STRIDE:
                z = z * after
            zcols[k, :, h * 128 : h * 128 + 128] = z.astype(BF16)

    jl = lax.broadcasted_iota(jnp.int32, (C, 384), 1) - GHALO
    alive = jnp.where(label(jl * STRIDE + anchor) >= 0, 1.0, 0.0)
    for o in range(2):
        g = gext_ref[o * C : (o + 1) * C, :].astype(F32) * alive
        gtf[8 : 8 + 384, o * C : (o + 1) * C] = g.T
    gtf[0:8, :] = jnp.zeros((8, 2 * C), F32)
    low = edge_mask(all_j, -GHALO, -1)
    high = edge_mask(all_j, -GHALO, STRIDE)
    for o in range(4):
        lanes = slice(o * 128, o * 128 + 128)
        gt[0, :, lanes] = gtf[8 : 8 + all_j, lanes].astype(BF16)
        gt[1, :, lanes] = (gtf[7 : 7 + all_j, lanes] * low).astype(BF16)
        gt[2, :, lanes] = (gtf[9 : 9 + all_j, lanes] * high).astype(BF16)

    for o in range(2):
        rows = slice(o * C, (o + 1) * C)
        total = dot_nt(wdn_ref[0, rows, :], zcols[0])
        for k in range(1, 2 * STRIDE):
            total = total + dot_nt(wdn_ref[k, rows, :], zcols[k])
        out_ref[rows, :] = total.astype(BF16)

    def stage_copy(k, slot):
        return pltpu.make_async_copy(stage.at[slot], gdn_ref.at[k], stage_sem.at[slot])

    own = gext_ref[:, GHALO : GHALO + rows_j]
    for k in range(2 * STRIDE):
        slot = k % 2
        if k >= 2:
            stage_copy(k - 2, slot).wait()
        stage[slot] = dot(own, zcols[k]).astype(stage.dtype)
        stage_copy(k, slot).start()
    for k in range(2 * STRIDE - 2, 2 * STRIDE):
        stage_copy(k, k % 2).wait()

    for p in range(STRIDE):
        if p < STRIDE // 2:
            d = dot(gt[1], wdn_ref[p + 12])
        else:
            d = dot(gt[2], wdn_ref[p - 4])
        d = d + dot(gt[0], wdn_ref[p + 4])
        for h in range(2):
            halves[h][pl.ds(p, all_j, stride=STRIDE), :] = d[:, h * 128 : h * 128 + 128]

    def dz_tile(j, own):
        src = pl.ds(pl.multiple_of(lax.rem(j + 1, tiles) * 128, 128), 128)
        dst = pl.ds(pl.multiple_of(j * 128, 128), 128)
        for h in range(2):
            rows = slice(h * 128, h * 128 + 128)
            dz = halves[h][src, :].T
            grad[rows, dst] = (dz * slope[4, rows, dst].astype(F32)).astype(BF16)
            if own:
                acc[4, rows, :] += dz * sa[4, rows, dst].astype(F32)

    lax.fori_loop(0, own_tiles, lambda j, _: (dz_tile(j, True), 0)[1], 0)
    for j in range(own_tiles, tiles):
        dz_tile(j, False)

    def backward(unit):
        cols, b_ref = cols_of[unit], b_of[unit]
        hi, ui = 2 * unit + 1, 2 * unit
        own_lanes = slice(0, samples)
        gw_ref[2 * TAPS + unit] = dot_nt(grad[:, own_lanes], b_ref[:, own_lanes]).astype(gw_ref.dtype)
        wpt[...] = wp_ref[unit].T
        for k in range(TAPS):
            wt[:, k * C : (k + 1) * C] = wd_ref[unit, :, (TAPS - 1 - k) * C : (TAPS - k) * C].T

        def hidden(nb, own):
            hbuf[...] = dot(wpt[...], grad[:, block_lanes(nb)])
            for r in range(0, C, 32):
                rows = slice(r, r + 32)
                for half in range(2):
                    hl = block_lanes(nb, half)
                    c = hbuf[rows, half * 128 : half * 128 + 128]
                    act[rows, hl] = (c * slope[hi, rows, hl].astype(F32)).astype(BF16)
                    if own:
                        acc[hi, rows, :] += c * sa[hi, rows, hl].astype(F32)

        over_blocks(hidden)

        def dilated(k, _):
            rows = pl.ds(pl.multiple_of(k * C, C), C)
            gw_ref[TAPS * unit + k] = dot_nt(act[:, own_lanes], cols[rows, own_lanes]).astype(gw_ref.dtype)
            return 0

        lax.fori_loop(0, TAPS, dilated, 0)
        shift_pass(act, cols, unit)

        def inner(nb, own):
            lanes = block_lanes(nb)
            hbuf[...] = dot(wt[...], cols[:, lanes])
            for r in range(0, C, 32):
                rows = slice(r, r + 32)
                for half in range(2):
                    hl = block_lanes(nb, half)
                    f = hbuf[rows, half * 128 : half * 128 + 128]
                    g = (grad[rows, hl].astype(F32) + f * slope[ui, rows, hl].astype(F32)).astype(BF16)
                    if unit == 0:
                        lv = live[:, hl]
                        sg_ref[rows, hl] = g * jnp.concatenate([lv, lv], axis=0)
                    else:
                        grad[rows, hl] = g
                    if own:
                        acc[ui, rows, :] += f * sa[ui, rows, hl].astype(F32)

        if unit == 0:
            lax.fori_loop(0, own_blocks, lambda nb, _: (inner(nb, True), 0)[1], 0)
        else:
            over_blocks(inner)

    backward(1)
    backward(0)
    ga_ref[...] = jnp.zeros_like(ga_ref)
    for i in range(5):
        ga_ref[i : i + 1, :] = jnp.sum(acc[i].T, axis=0, keepdims=True)


def compute(lengths, sig, gext, conv_dilated, conv_point, conv_down, snake_alpha, samples):
    extent = samples + 2 * HALO
    rows_j = samples // STRIDE
    all_j = extent // STRIDE
    vmem = pl.BlockSpec(memory_space=pltpu.VMEM)
    outs = (
        jax.ShapeDtypeStruct((2 * C, rows_j), BF16),
        jax.ShapeDtypeStruct((C, samples), BF16),
        jax.ShapeDtypeStruct((2 * TAPS + 2, C, C), BF16),
        jax.ShapeDtypeStruct((2 * STRIDE, 2 * C, C), BF16),
        jax.ShapeDtypeStruct((8, C), F32),
    )
    scratch = [
        pltpu.VMEM((TAPS * C, extent), BF16),
        pltpu.VMEM((TAPS * C, extent), BF16),
        pltpu.VMEM((C, extent), BF16),
        pltpu.VMEM((C, extent), BF16),
        pltpu.VMEM((C, extent), BF16),
        pltpu.VMEM((C, extent), BF16),
        pltpu.VMEM((C, extent), BF16),
        pltpu.VMEM((C, extent), BF16),
        pltpu.VMEM((5, C, extent), BF16),
        pltpu.VMEM((5, C, samples), BF16),
        pltpu.VMEM((extent, 128), F32),
        pltpu.VMEM((extent, 128), F32),
        pltpu.VMEM((2 * STRIDE, rows_j, C), BF16),
        pltpu.VMEM((400, 2 * C), F32),
        pltpu.VMEM((3, all_j, 2 * C), BF16),
        pltpu.VMEM((C, TAPS * C), BF16),
        pltpu.VMEM((C, C), BF16),
        pltpu.VMEM((2 * (TAPS - 1), 16, extent), BF16),
        pltpu.VMEM((16, extent), BF16),
        pltpu.VMEM((2, 5, C, 128), F32),
        pltpu.VMEM((5, C, 128), F32),
        pltpu.VMEM((C, BLOCK), F32),
        pltpu.VMEM((2, 2 * C, C), BF16),
        pltpu.SemaphoreType.DMA((2,)),
    ]
    return pl.pallas_call(
        functools.partial(compute_kernel, samples),
        out_shape=outs,
        in_specs=[pl.BlockSpec(memory_space=pltpu.SMEM)] + [vmem] * 6,
        out_specs=(vmem, vmem, vmem, pl.BlockSpec(memory_space=pl.ANY), vmem),
        scratch_shapes=scratch,
        compiler_params=pltpu.CompilerParams(vmem_limit_bytes=63 * 1024 * 1024),
        name="encoder_block",
    )(lengths, sig, gext, conv_dilated, conv_point, conv_down, snake_alpha)


RING = 4
PARTS = 3
MESH = pl.DeviceIdType.MESH


def sum_kernel(gdn_ref, gw_ref, ga_ref, fdn_ref, fw_ref, gao_ref, own, w, pr, ra, rb, gr, gat,
               own_sem, pair_s, pair_r, rs_s, rs_r, ag_s, ag_r, back_s, back_r, ga_s, ga_r):
    part = gw_ref.shape[0] // 2
    chunk = part // RING
    dp, tm = lax.axis_index("dp"), lax.axis_index("tm")
    core, y = lax.rem(dp, 2), dp // 2
    x, z = lax.rem(tm, RING), tm // RING
    place = (x, y, z)

    def wrap(c):
        return lax.rem(c + RING, RING)

    def device(axis, coord):
        xyz = [wrap(coord) if a == axis else place[a] for a in range(3)]
        return (xyz[1] * 2 + core, xyz[2] * RING + xyz[0])

    sibling = (y * 2 + 1 - core, tm)
    barrier = pltpu.get_barrier_semaphore()
    peers = [sibling] + [device(a, place[a] + s) for a in range(3) for s in (1, 2, 3)]
    for peer in peers:
        pl.semaphore_signal(barrier, inc=1, device_id=peer, device_id_type=MESH)
    pl.semaphore_wait(barrier, len(peers))

    sends = []

    def remote(src, dst, send_sem, recv_sem, dev):
        return pltpu.make_async_remote_copy(
            src_ref=src, dst_ref=dst, send_sem=send_sem, recv_sem=recv_sem,
            device_id=dev, device_id_type=MESH,
        )

    def send(*args):
        copy = remote(*args)
        copy.start()
        sends.append(copy)

    def at(ref, start, count):
        return ref.at[pl.ds(pl.multiple_of(start, 16), count), :]

    def part_of(p, hf, refs):
        return (refs[0], hf * 2 * part + p * part) if p < 2 else (refs[1], hf * part)

    def grads(p, hf, row):
        ref, first = part_of(p, hf, (gdn_ref, gw_ref))
        return at(ref, first + row, chunk)

    def result(p, hf, row, count):
        ref, first = part_of(p, hf, (fdn_ref, fw_ref))
        return at(ref, first + row, count)

    def axis_of(p, s):
        return (p + s) % 3

    def add_rows(dst, d0, terms, count):
        step = min(count, 64)

        def one(i, _):
            v = None
            for ref, r0 in terms:
                t = ref[pl.ds(pl.multiple_of(r0 + i * step, 16), step), :].astype(F32)
                v = t if v is None else v + t
            dst[pl.ds(pl.multiple_of(d0 + i * step, 16), step), :] = v.astype(dst.dtype)
            return 0

        lax.fori_loop(0, count // step, one, 0)

    send(ga_ref, gr.at[3, 0], ga_s.at[3, 0], ga_r.at[3, 0], sibling)

    def ga_step(s):
        if s == 0:
            remote(ga_ref, gr.at[3, 0], ga_s.at[3, 0], ga_r.at[3, 0], sibling).wait_recv()
            gat[0] = ga_ref[...] + gr[3, 0]
        else:
            ga_wait(s - 1)
        me = place[s]
        gr[s, me] = gat[s]
        for k in range(1, RING):
            send(gat.at[s], gr.at[s, me], ga_s.at[s, k], ga_r.at[s, k], device(s, me + k))

    def ga_wait(s):
        me = place[s]
        for k in range(1, RING):
            src = wrap(me - k)
            remote(gat.at[s], gr.at[s, src], ga_s.at[s, k], ga_r.at[s, k], device(s, src)).wait_recv()
        gat[s + 1] = (gr[s, 0] + gr[s, 1]) + (gr[s, 2] + gr[s, 3])

    order = (2, 1, 3, 0)
    for o, off in enumerate(order):
        for p in range(PARTS):
            i = o * PARTS + p
            row = wrap(place[axis_of(p, 0)] + off) * chunk
            send(grads(p, 1 - core, row), at(pr.at[p], row, chunk), pair_s.at[i], pair_r.at[i], sibling)
    for o, off in enumerate(order):
        for p in range(PARTS):
            i = o * PARTS + p
            row = wrap(place[axis_of(p, 0)] + off) * chunk
            pltpu.make_async_copy(grads(p, core, row), at(own.at[p], row, chunk), own_sem.at[i]).start()

    def pair_wait(o, p):
        i = o * PARTS + p
        row = wrap(place[axis_of(p, 0)] + order[o]) * chunk
        pltpu.make_async_copy(grads(p, core, row), at(own.at[p], row, chunk), own_sem.at[i]).wait()
        land = at(pr.at[p], row, chunk)
        remote(land, land, pair_s.at[i], pair_r.at[i], sibling).wait_recv()
        add_rows(w.at[p], row, ((own.at[p], row), (pr.at[p], row)), chunk)

    base = [0] * PARTS
    bases = []
    ra_at, rb_at = 0, 0
    for s in range(3):
        q = part // RING ** (s + 1)
        h = q // 2
        bases.append(list(base))
        for p in range(PARTS):
            if s == 0:
                pair_wait(0, p)
            a = axis_of(p, s)
            for d, sign in enumerate((1, -1)):
                i = ((p * 3 + s) * 2) * 2 + d
                send(at(w.at[p], base[p] + wrap(place[a] + 2) * q + d * h, h), at(ra.at[p], ra_at + d * h, h),
                     rs_s.at[i], rs_r.at[i], device(a, place[a] + sign))
        for d, sign in enumerate((1, -1)):
            for p in range(PARTS):
                if s == 0:
                    pair_wait(1 + d, p)
                a = axis_of(p, s)
                here = base[p] + wrap(place[a] + sign) * q
                to = device(a, place[a] + sign)
                i = ((p * 3 + s) * 2) * 2 + d
                land = at(ra.at[p], ra_at + d * h, h)
                remote(land, land, rs_s.at[i], rs_r.at[i], to).wait_recv()
                add_rows(w.at[p], here + d * h, ((w.at[p], here + d * h), (ra.at[p], ra_at + d * h)), h)
                i += 2
                send(at(w.at[p], here, q), at(rb.at[p], rb_at + d * q, q), rs_s.at[i], rs_r.at[i], to)
        ga_step(s)
        for p in range(PARTS):
            if s == 0:
                pair_wait(3, p)
            a = axis_of(p, s)
            for d, sign in enumerate((1, -1)):
                i = ((p * 3 + s) * 2 + 1) * 2 + d
                land = at(rb.at[p], rb_at + d * q, q)
                remote(land, land, rs_s.at[i], rs_r.at[i], device(a, place[a] + sign)).wait_recv()
            here = base[p] + place[a] * q
            terms = ((w.at[p], here), (rb.at[p], rb_at), (rb.at[p], rb_at + q))
            if s < 2:
                add_rows(w.at[p], here, terms, q)
            else:
                ref, first = part_of(p, core, (fdn_ref, fw_ref))
                add_rows(ref, first + here, terms, q)
            base[p] = here
        ra_at, rb_at = ra_at + 2 * h, rb_at + 2 * q

    def back(n, p, c):
        i = n * PARTS + p
        piece = result(p, core, c * chunk, chunk)
        send(piece, piece, back_s.at[i], back_r.at[i], sibling)

    for s in (2, 1, 0):
        q = part // RING ** (s + 1)
        h = q // 2
        for p in range(PARTS):
            a = axis_of(p, s)
            block = result(p, core, bases[s][p] + place[a] * q, q)
            for d, sign in enumerate((1, -1)):
                i = ((p * 3 + s) * 2) * 2 + d
                send(block, block, ag_s.at[i], ag_r.at[i], device(a, place[a] + sign))
        if s == 0:
            for p in range(PARTS):
                back(0, p, place[axis_of(p, 0)])
        for d, sign in enumerate((1, -1)):
            for p in range(PARTS):
                a = axis_of(p, s)
                i = ((p * 3 + s) * 2) * 2 + d
                c = wrap(place[a] - sign)
                to = device(a, place[a] + sign)
                block = result(p, core, bases[s][p] + c * q, q)
                remote(block, block, ag_s.at[i], ag_r.at[i], to).wait_recv()
                i += 2
                piece = result(p, core, bases[s][p] + c * q + d * h, h)
                send(piece, piece, ag_s.at[i], ag_r.at[i], to)
                if s == 0:
                    back(1 + d, p, c)
        for p in range(PARTS):
            a = axis_of(p, s)
            c = wrap(place[a] + 2)
            for d, sign in enumerate((1, -1)):
                i = ((p * 3 + s) * 2 + 1) * 2 + d
                piece = result(p, core, bases[s][p] + c * q + d * h, h)
                remote(piece, piece, ag_s.at[i], ag_r.at[i], device(a, place[a] + sign)).wait_recv()
            if s == 0:
                back(3, p, c)
    ga_wait(2)
    gao_ref[...] = gat[3]
    for n, off in enumerate((0, -1, 1, 2)):
        for p in range(PARTS):
            i = n * PARTS + p
            piece = result(p, 1 - core, wrap(place[axis_of(p, 0)] + off) * chunk, chunk)
            remote(piece, piece, back_s.at[i], back_r.at[i], sibling).wait_recv()
    for copy in sends:
        copy.wait_send()


def sum_over_devices(gdn, gw, ga):
    part = gw.shape[0] // 2
    vmem = pl.BlockSpec(memory_space=pltpu.VMEM)
    anywhere = pl.BlockSpec(memory_space=pl.ANY)
    dma = pltpu.SemaphoreType.DMA
    gathered = sum(part // RING ** (s + 1) for s in range(3))
    return pl.pallas_call(
        sum_kernel,
        out_shape=(
            jax.ShapeDtypeStruct(gdn.shape, BF16),
            jax.ShapeDtypeStruct(gw.shape, BF16),
            jax.ShapeDtypeStruct(ga.shape, F32),
        ),
        in_specs=[anywhere, anywhere, vmem],
        out_specs=(vmem, vmem, vmem),
        scratch_shapes=[
            pltpu.VMEM((PARTS, part, C), BF16),
            pltpu.VMEM((PARTS, part, C), BF16),
            pltpu.VMEM((PARTS, part, C), BF16),
            pltpu.VMEM((PARTS, gathered, C), BF16),
            pltpu.VMEM((PARTS, 2 * gathered, C), BF16),
            pltpu.VMEM((4, RING) + ga.shape, F32),
            pltpu.VMEM((4,) + ga.shape, F32),
            dma((4 * PARTS,)), dma((4 * PARTS,)), dma((4 * PARTS,)),
            dma((12 * PARTS,)), dma((12 * PARTS,)), dma((12 * PARTS,)), dma((12 * PARTS,)),
            dma((4 * PARTS,)), dma((4 * PARTS,)),
            dma((4, RING)), dma((4, RING)),
        ],
        compiler_params=pltpu.CompilerParams(
            collective_id=1, has_side_effects=True, vmem_limit_bytes=40 * 1024 * 1024
        ),
        name="sum_over_devices",
    )(gdn, gw, ga)


def body(signal, lengths, conv_dilated, conv_point, conv_down, snake_alpha, out_grad):
    samples = signal.shape[2]
    sig, og = signal[0], out_grad[0]
    count = lax.axis_size("tm")
    forward = [(i, i + 1) for i in range(count - 1)]
    backward = [(b, a) for a, b in forward]
    left = lax.ppermute(sig[:, -HALO:], "tm", forward)
    right = lax.ppermute(sig[:, :HALO], "tm", backward)
    gleft = lax.ppermute(og[:, -GHALO:], "tm", forward)
    gright = lax.ppermute(og[:, :GHALO], "tm", backward)
    ext = jnp.concatenate([sig, right, left], axis=1)
    pad = jnp.zeros((og.shape[0], 128 - 2 * GHALO), og.dtype)
    gext = jnp.concatenate([gleft, og, gright, pad], axis=1)
    out, sg, gw, gdn, ga = compute(
        lengths, ext, gext, conv_dilated, conv_point, conv_down, snake_alpha, samples
    )
    fdn, fw, ga = sum_over_devices(gdn.reshape(-1, C), gw.reshape(-1, C), ga)
    fw = fw.reshape(gw.shape)
    gd = fw[: 2 * TAPS].reshape(2, TAPS, C, C).transpose(0, 2, 1, 3).reshape(2, C, TAPS * C)
    gp = fw[2 * TAPS :]
    return (
        out[None],
        sg[None],
        gd.astype(F32),
        gp.astype(F32),
        fdn.reshape(gdn.shape).astype(F32),
        ga[:5],
    )


def solution(mesh):
    placed = (P("dp", None, "tm"), P("dp", None), P(), P(), P(), P(), P("dp", None, "tm"))
    return jax.shard_map(
        body,
        mesh=mesh,
        in_specs=placed,
        out_specs=(P("dp", None, "tm"), P("dp", None, "tm"), P(), P(), P(), P()),
        check_vma=False,
    )
```

```python
import functools

import jax
import jax.numpy as jnp
from jax import lax
from jax.experimental import pallas as pl
from jax.experimental.pallas import tpu as pltpu
from jax.sharding import PartitionSpec as P

TAPS = 7
STRIDE = 8
DILATIONS = (3, 9)
TILE = 64
REC = 4
C = 256
LEAD = 112
F32 = jnp.float32
BF16 = jnp.bfloat16

SIN_PI = (3.14158202, -5.16714279, 2.54189898, -0.55463609)
TWO_COS_PI = (1.9999999, -9.86958572, 8.11682382, -2.66376026, 0.43939346)


def dot(a, b):
    return jnp.dot(a, b, preferred_element_type=F32)


def dot_nt(a, b):
    return lax.dot_general(a, b, (((1,), (1,)), ((), ())), preferred_element_type=F32)


def poly(coefs, x):
    total = coefs[-1]
    for c in coefs[-2::-1]:
        total = total * x + c
    return total


def sine_parts(turns):
    f = turns - jnp.round(turns)
    x = f * f
    s = f * poly(SIN_PI, x)
    return s * poly(TWO_COS_PI, x), s * s


RING = 4
MESH = pl.DeviceIdType.MESH
ORDERS = ((0, 1, 2), (1, 2, 0), (2, 0, 1), (0, 2, 1), (1, 2, 0), (2, 0, 1), (1, 2, 0), (2, 0, 1))
JOB_ROWS = (2048,) * 4 + (1024,) * 4


class Links:
    def __init__(self):
        self.dp, self.tm = lax.axis_index("dp"), lax.axis_index("tm")
        self.core = lax.rem(self.dp, 2)
        self.place = (lax.rem(self.tm, RING), self.dp // 2, self.tm // RING)
        self.sibling = (self.dp + 1 - 2 * self.core, self.tm)
        self.sends = []

    def along(self, axis, step):
        x, y, z = (
            lax.rem(c + step + RING, RING) if a == axis else c for a, c in enumerate(self.place)
        )
        return (y * 2 + self.core, z * RING + x)

    def in_time(self, step):
        count = lax.axis_size("tm")
        return (self.dp, lax.rem(self.tm + step + count, count))

    def peers(self):
        ring = [self.along(a, s) for a in range(3) for s in (1, 2, 3)]
        return [self.sibling, self.in_time(1), self.in_time(-1)] + ring

    def greet(self):
        barrier = pltpu.get_barrier_semaphore()
        for peer in self.peers():
            pl.semaphore_signal(barrier, inc=1, device_id=peer, device_id_type=MESH)

    def met(self):
        pl.semaphore_wait(pltpu.get_barrier_semaphore(), len(self.peers()))

    def remote(self, src, dst, send_sem, recv_sem, dev):
        return pltpu.make_async_remote_copy(
            src_ref=src, dst_ref=dst, send_sem=send_sem, recv_sem=recv_sem,
            device_id=dev, device_id_type=MESH,
        )

    def send(self, *args):
        copy = self.remote(*args)
        copy.start()
        self.sends.append(copy)

    def drain(self):
        for copy in self.sends:
            copy.wait_send()


def block_kernel(samples, len_ref, sig_ref, og_ref, wd_ref, wp_ref, wdn_hbm, al_ref,
                 out_ref, sg_ref, fdn_ref, fw_ref, fa_ref,
                 cols, af0, af1, df0, df1, u0, u1, a0, b0, b1, grad, slope, sa, tr, zcols,
                 gb, gtf, gt, wt, wpt, rem, kcol, acc, hbuf, wdn_ref, gdn, gw, ga,
                 pr_dn, pr_w, land_dn, land_w, fin, gr, gat,
                 load_sem, halo_s, halo_r, pair_s, pair_r, rs_s, rs_r, ag_s, ag_r, fin_sem, back_s, back_r, ga_s, ga_r):
    load = pltpu.make_async_copy(wdn_hbm, wdn_ref, load_sem)
    load.start()
    links = Links()
    links.greet()
    jobs = []

    def tick():
        for job in list(jobs):
            if next(job, True):
                jobs.remove(job)

    u_of, b_of = (u0, u1), (b0, b1)
    af, df = (af0, af1), (df0, df1)
    rows_all = u0.shape[0]
    own0, own1 = LEAD, LEAD + samples
    wide = (own0 - 64, own1 + 64)
    near = (own0 - 32, own1 + 32)
    own_rows = (own0, own1)
    rows_j = samples // STRIDE
    all_j = rows_j + 16
    anchor = lax.axis_index("tm") * samples
    halves = (slice(0, 128), slice(128, 256))

    core = links.core
    place = links.place

    def job_rows(p, hf):
        if p < 4:
            return gdn, fdn_ref, hf * 4 * JOB_ROWS[0] + p * JOB_ROWS[0]
        unit, sub = (p - 4) // 2, (p - 4) % 2
        return gw, fw_ref, (unit * 4 + hf * 2 + sub) * JOB_ROWS[4]

    def at(ref, start, count):
        return ref.at[pl.ds(pl.multiple_of(start, 16), count), :]

    def wrap(c):
        return lax.rem(c + RING, RING)

    def add_rows(dst, d0, terms, count):
        step_rows = min(count, 128)

        def one(i, _):
            v = None
            for ref, r0 in terms:
                t = ref[pl.ds(pl.multiple_of(r0 + i * step_rows, 16), step_rows), :].astype(F32)
                v = t if v is None else v + t
            dst[pl.ds(pl.multiple_of(d0 + i * step_rows, 16), step_rows), :] = v.astype(dst.dtype)
            return 0

        lax.fori_loop(0, count // step_rows, one, 0)

    def job(p):
        axes = ORDERS[p]
        part = JOB_ROWS[p]
        chunk = part // RING
        src, res, other_row = job_rows(p, 1 - core)
        own_row = job_rows(p, core)[2]
        w, land = (pr_dn.at[p], land_dn.at[p]) if p < 4 else (pr_w.at[p - 4], land_w.at[p - 4])
        last = fin.at[p, 0 : part // RING**3, :]
        ring_first = p < 4

        def result(row, count):
            return at(res, own_row + row, count)

        def rs(s, i):
            return rs_s.at[(p * 3 + s) * 4 + i], rs_r.at[(p * 3 + s) * 4 + i]

        def ag(s, i):
            return ag_s.at[(p * 3 + s) * 4 + i], ag_r.at[(p * 3 + s) * 4 + i]

        links.send(at(src, other_row, part), w, pair_s.at[p], pair_r.at[p], links.sibling)
        yield False
        links.remote(w, w, pair_s.at[p], pair_r.at[p], links.sibling).wait_recv()
        add_rows(w, 0, ((w, 0), (src, own_row)), part)
        base, bases, free = 0, [], 0
        for s in range(3):
            q = part // RING ** (s + 1)
            h = q // 2
            me = place[axes[s]]
            bases.append(base)
            here = base + me * q
            if s == 0 and ring_first:
                for d, sign in enumerate((1, -1)):
                    links.send(at(w, base + wrap(me + 2) * q + d * h, h), land.at[free + d * h : free + d * h + h, :],
                               *rs(s, d), links.along(axes[s], sign))
                yield False
                for d, sign in enumerate((1, -1)):
                    to = links.along(axes[s], sign)
                    row = base + wrap(me + sign) * q
                    half = land.at[free + d * h : free + d * h + h, :]
                    links.remote(half, half, *rs(s, d), to).wait_recv()
                    add_rows(w, row + d * h, ((w, row + d * h), (land, free + d * h)), h)
                    whole = land.at[free + (d + 1) * q : free + (d + 2) * q, :]
                    links.send(at(w, row, q), whole, *rs(s, 2 + d), to)
                yield False
                for d, sign in enumerate((1, -1)):
                    whole = land.at[free + (d + 1) * q : free + (d + 2) * q, :]
                    links.remote(whole, whole, *rs(s, 2 + d), links.along(axes[s], sign)).wait_recv()
                terms = ((w, here), (land, free + q), (land, free + 2 * q))
            else:
                for k in (2, 1, 3):
                    links.send(at(w, base + wrap(me + k) * q, q), land.at[free + (k - 1) * q : free + k * q, :],
                               *rs(s, k), links.along(axes[s], k))
                yield False
                for k in (1, 3, 2):
                    whole = land.at[free + (k - 1) * q : free + k * q, :]
                    links.remote(whole, whole, *rs(s, k), links.along(axes[s], k)).wait_recv()
                terms = ((w, here),) + tuple((land, free + i * q) for i in range(3))
            if s < 2:
                add_rows(w, here, terms, q)
            else:
                add_rows(last, 0, terms, q)
            base = here
            free += 3 * q
        keep_fin = pltpu.make_async_copy(last, result(base, q), fin_sem.at[p])
        keep_fin.start()
        for s in (2, 1, 0):
            q = part // RING ** (s + 1)
            h = q // 2
            me = place[axes[s]]
            block = result(bases[s] + me * q, q)
            if s == 0:
                links.send(block, block, back_s.at[p, 0], back_r.at[p, 0], links.sibling)
            if s == 0 and ring_first:
                for d, sign in enumerate((1, -1)):
                    links.send(block, block, *ag(s, d), links.along(axes[s], sign))
                yield False
                for d, sign in enumerate((1, -1)):
                    to = links.along(axes[s], sign)
                    row = bases[s] + wrap(me - sign) * q
                    block = result(row, q)
                    links.remote(block, block, *ag(s, d), to).wait_recv()
                    piece = result(row + d * h, h)
                    links.send(piece, piece, *ag(s, 2 + d), to)
                    links.send(block, block, back_s.at[p, 1 + d], back_r.at[p, 1 + d], links.sibling)
                yield False
                row = bases[s] + wrap(me + 2) * q
                for d, sign in enumerate((1, -1)):
                    piece = result(row + d * h, h)
                    links.remote(piece, piece, *ag(s, 2 + d), links.along(axes[s], sign)).wait_recv()
                block = result(row, q)
                links.send(block, block, back_s.at[p, 3], back_r.at[p, 3], links.sibling)
            else:
                for k in (2, 1, 3):
                    links.send(last if s == 2 else block, block, *ag(s, k), links.along(axes[s], k))
                yield False
                for i, k in enumerate((1, 3, 2)):
                    block = result(bases[s] + wrap(me - k) * q, q)
                    links.remote(block, block, *ag(s, k), links.along(axes[s], k)).wait_recv()
                    if s == 0:
                        links.send(block, block, back_s.at[p, 1 + i], back_r.at[p, 1 + i], links.sibling)
            if s == 2:
                keep_fin.wait()
        yield False
        for i, off in enumerate((0, -1, 1, 2)):
            piece = at(res, other_row + wrap(place[axes[0]] + off) * chunk, chunk)
            links.remote(piece, piece, back_s.at[p, i], back_r.at[p, i], links.sibling).wait_recv()
        yield True

    def alpha_job():
        links.send(ga, gr.at[3, 0], ga_s.at[3, 0], ga_r.at[3, 0], links.sibling)
        yield False
        links.remote(ga, gr.at[3, 0], ga_s.at[3, 0], ga_r.at[3, 0], links.sibling).wait_recv()
        gat[0] = ga[...] + gr[3, 0]
        for s in range(3):
            me = place[s]
            gr[s, me] = gat[s]
            for k in range(1, RING):
                links.send(gat.at[s], gr.at[s, me], ga_s.at[s, k], ga_r.at[s, k], links.along(s, k))
            yield False
            for k in range(1, RING):
                links.remote(gat.at[s], gr.at[s, wrap(me - k)], ga_s.at[s, k], ga_r.at[s, k],
                             links.along(s, k)).wait_recv()
            gat[s + 1] = (gr[s, 0] + gr[s, 1]) + (gr[s, 2] + gr[s, 3])
        fa_ref[...] = gat[3]
        yield True

    ends = []
    total = 0
    for r in range(REC):
        total = total + len_ref[0, r]
        ends.append(total * TILE)

    def rem_body(i, _):
        rows = pl.ds(pl.multiple_of(i * 32, 32), 32)
        p = lax.broadcasted_iota(jnp.int32, (32, 128), 0) + (i * 32 - LEAD + anchor)
        hi, lo = jnp.zeros_like(p), jnp.full_like(p, -1)
        start = 0
        for end in ends:
            inside = (p >= start) & (p < end)
            hi = jnp.where(inside, end - p, hi)
            lo = jnp.where(inside, p - start, lo)
            start = end
        rem[0, rows, :] = hi
        rem[1, rows, :] = lo
        return 0

    lax.fori_loop(0, rows_all // 32, rem_body, 0)

    for i in range(5):
        row = jnp.broadcast_to(al_ref[i : i + 1, :], (8, C))
        for h in range(2):
            kcol[0, i, h] = row[:, halves[h]] * (1.0 / 3.14159265358979)
            kcol[1, i, h] = 1.0 / row[:, halves[h]]
    acc[...] = jnp.zeros_like(acc)

    def four(x):
        return jnp.concatenate([x] * 4, axis=0)

    def activate(v, i, h):
        k0 = four(kcol[0, i, h])
        k1 = four(kcol[1, i, h])
        s2, sq = sine_parts(v * k0)
        q = sq * k1
        return v + q, s2, v * s2 - q

    class Totals:
        def __init__(self, i):
            self.i, self.sums = i, [None, None]

        def add(self, h, x):
            x = (x[0:8] + x[8:16]) + (x[16:24] + x[24:32])
            self.sums[h] = x if self.sums[h] is None else self.sums[h] + x

        def store(self):
            for h in range(2):
                if self.sums[h] is not None:
                    acc[self.i, h] += self.sums[h]

    def pieces(lo, hi):
        return [(slice(r, r + 32), r - lo, own0 <= r and r + 32 <= own1) for r in range(lo, hi, 32)]

    def row_loop(lo, hi, fn, group=4):
        cuts = sorted({lo, max(lo, own0), min(hi, own1), hi})
        for a, b in zip(cuts, cuts[1:]):
            own = a >= own0 and b <= own1
            many = group if ((b - a) // 32) % group == 0 else 1

            def step(i, _, own=own, a=a, many=many):
                for n in range(many):
                    fn(pl.ds(pl.multiple_of((i * many + n) * 32 + a, 16), 32), own)
                return 0

            lax.fori_loop(0, (b - a) // (32 * many), step, 0)

    def pipelined(span, blocks, product, use, mid=False):
        lo, hi = span
        count = (hi - lo) // 32
        starts = [lo + 32 * (count * n // blocks) for n in range(blocks + 1)]
        spans = list(zip(starts, starts[1:]))

        def make(n):
            a, b = spans[n]
            hbuf[n % 2, 0 : b - a, :] = product(slice(a, b))

        make(0)
        for n, (a, b) in enumerate(spans):
            if n + 1 < blocks:
                make(n + 1)
            use(pieces(a, b), hbuf.at[n % 2])
            if n == 1 and mid:
                tick()

    def forward_weights(unit):
        for k in range(TAPS):
            wt[k * C : (k + 1) * C, :] = wd_ref[unit, :, k * C : (k + 1) * C].T
        wpt[...] = wp_ref[unit].T

    def sig_body(j, _):
        src = pl.ds(pl.multiple_of(j * 512, 128), 512)
        u0[pl.ds(pl.multiple_of(j * 512 + own0, 16), 512), :] = sig_ref[:, src].T
        return 0

    lax.fori_loop(0, samples // 512, sig_body, 0)
    for o in range(2):
        gb[16 : 16 + rows_j, o * C : (o + 1) * C] = og_ref[o * C : (o + 1) * C, :].T

    links.met()
    halo = []
    for i, (ref, count, first, last) in enumerate(((u0, 80, own0, own1), (gb, 16, 16, 16 + rows_j))):
        for side, (step, src, dst) in enumerate(((-1, first, last), (1, last - count, first - count))):
            n = 2 * i + side
            halo.append(links.remote(ref.at[src : src + count, :], ref.at[dst : dst + count, :],
                                     halo_s.at[n], halo_r.at[n], links.in_time(step)))
    for copy in halo:
        copy.start()
    for h in range(2):
        af[h][...] = jnp.zeros_like(af[h])
        df[h][...] = jnp.zeros_like(df[h])
    forward_weights(0)
    for copy in halo:
        copy.wait()

    def keep(i, rows, h, s2, t):
        slope[i, rows, halves[h]] = (1.0 + s2).astype(BF16)
        sa[i, rows, halves[h]] = t.astype(BF16)

    def first(rows, own):
        alive = rem[0, rows, :] > 0
        for h in range(2):
            v = jnp.where(alive, u0[rows, halves[h]].astype(F32), 0.0)
            u0[rows, halves[h]] = v.astype(BF16)
            a, s2, t = activate(v, 0, h)
            af[h][rows, :] = a
            a0[rows, halves[h]] = a.astype(BF16)
            keep(0, rows, h, s2, t)

    row_loop(own0 - 64 - 32, own1 + 64 + 32, first)

    def shift_pass(unit, span):
        d = DILATIONS[unit]
        lo, hi = span

        def step(i, _):
            start = i * 32 + lo
            rows = pl.ds(pl.multiple_of(start, 16), 32)
            after, before = rem[0, rows, :], rem[1, rows, :]
            for k in range(TAPS):
                by = (k - TAPS // 2) * d
                for h in range(2):
                    x = af[h][pl.ds(start + by, 32), :]
                    if by > 0:
                        x = jnp.where(after > by, x, 0.0)
                    elif by < 0:
                        x = jnp.where(before >= -by, x, 0.0)
                    cols[rows, k * C + h * 128 : k * C + h * 128 + 128] = x.astype(BF16)
            return 0

        lax.fori_loop(0, (hi - lo) // 32, step, 0)

    def forward(unit):
        b_ref, u_ref = b_of[unit], u_of[unit]
        hi, ui = 2 * unit + 1, 2 * unit + 2
        def hidden(parts, buf):
            for r, o, own in parts:
                for h in range(2):
                    a, s2, t = activate(buf[o : o + 32, halves[h]], hi, h)
                    b_ref[r, halves[h]] = a.astype(BF16)
                    keep(hi, r, h, s2, t)

        pipelined(wide, 4, lambda rows: dot(cols[rows, :], wt[...]), hidden)

        def outer(parts, buf):
            for r, o, own in parts:
                for h in range(2):
                    u = (u_ref[r, halves[h]].astype(F32) + buf[o : o + 32, halves[h]]).astype(BF16)
                    if unit == 0:
                        u1[r, halves[h]] = u
                    a, s2, t = activate(u.astype(F32), ui, h)
                    af[h][r, :] = a
                    keep(ui, r, h, s2, t)

        pipelined(wide, 4, lambda rows: dot(b_ref[rows, :], wpt[...]), outer)

    shift_pass(0, wide)
    forward(0)
    forward_weights(1)
    shift_pass(1, wide)
    forward(1)

    at_j = pl.ds(own0, rows_j, stride=STRIDE)
    after, before = rem[0, at_j, :], rem[1, at_j, :]
    for k in range(2 * STRIDE):
        by = k - STRIDE // 2
        for h in range(2):
            z = af[h][pl.ds(own0 + by, rows_j, stride=STRIDE), :]
            if by < 0:
                z = jnp.where(before >= -by, z, 0.0)
            elif by >= STRIDE:
                z = jnp.where(after > by, z, 0.0)
            zcols[k, :, halves[h]] = z.astype(BF16)

    gtf[8 : 8 + rows_j + 32, :] = gb[...].astype(F32)
    at_m = pl.ds(wide[0], all_j, stride=STRIDE)
    after, before = rem[0, at_m, :], rem[1, at_m, :]
    for o in range(4):
        lanes = slice(o * 128, o * 128 + 128)
        gt[0, :, lanes] = jnp.where(after > 0, gtf[16 : 16 + all_j, lanes], 0.0).astype(BF16)
        gt[1, :, lanes] = jnp.where(before > 0, gtf[15 : 15 + all_j, lanes], 0.0).astype(BF16)
        gt[2, :, lanes] = jnp.where(after > STRIDE, gtf[17 : 17 + all_j, lanes], 0.0).astype(BF16)

    load.wait()

    own = og_ref[...]

    def down_body(k, _):
        d = dot(own, zcols[k]).astype(BF16)
        for h in range(2):
            gdn[pl.ds(pl.multiple_of((2 * k + h) * 2 * C, 16), 2 * C), :] = d[:, halves[h]]
        return 0

    lax.fori_loop(0, 2 * STRIDE, down_body, 0)
    for p in range(4):
        jobs.append(job(p))
    tick()

    for o in range(2):
        rows = slice(o * C, (o + 1) * C)
        total = dot_nt(wdn_ref[0, rows, :], zcols[0])
        for k in range(1, 2 * STRIDE):
            total = total + dot_nt(wdn_ref[k, rows, :], zcols[k])
        out_ref[rows, :] = total.astype(BF16)
    tick()

    for p in range(STRIDE):
        if p < STRIDE // 2:
            d = dot(gt[1], wdn_ref[p + 12])
        else:
            d = dot(gt[2], wdn_ref[p - 4])
        d = d + dot(gt[0], wdn_ref[p + 4])
        for h in range(2):
            df[h][pl.ds(wide[0] + p, all_j, stride=STRIDE), :] = d[:, halves[h]]
    tick()

    sums = Totals(4)
    for r, _, own_piece in pieces(*wide):
        for h in range(2):
            dz = df[h][r, :]
            grad[r, halves[h]] = (dz * slope[4, r, halves[h]].astype(F32)).astype(BF16)
            if own_piece:
                sums.add(h, dz * sa[4, r, halves[h]].astype(F32))
    sums.store()

    def transposed(j, _):
        lanes = pl.ds(pl.multiple_of(j * 512, 128), 512)
        tr[:, lanes] = grad[pl.ds(pl.multiple_of(j * 512 + own0, 16), 512), :].T
        return 0

    def transposed_e(j, _):
        lanes = pl.ds(pl.multiple_of(j * 512, 128), 512)
        rows = pl.ds(pl.multiple_of(j * 512 + own0, 16), 512)
        for h in range(2):
            tr[halves[h], lanes] = af[h][rows, :].astype(BF16).T
        return 0

    def put_gw(unit, k, x):
        for h in range(2):
            first = ((unit * (TAPS + 1) + k) * 2 + h) * C
            gw[first : first + C, :] = x[:, halves[h]].astype(BF16)

    def backward(unit):
        b_ref = b_of[unit]
        hi, ui = 2 * unit + 1, 2 * unit
        span = (near, wide)[unit]
        lax.fori_loop(0, samples // 512, transposed, 0)
        put_gw(unit, TAPS, dot(tr[...], b_ref[own0:own1, :]))
        if unit == 1:
            tick()
        if unit == 0:

            def again(rows, own):
                for h in range(2):
                    af[h][rows, :] = a0[rows, halves[h]].astype(F32)

            row_loop(*near, again)
            shift_pass(0, own_rows)
            tick()

        def hidden(parts, buf):
            sums = Totals(hi)
            for r, o, own in parts:
                for h in range(2):
                    c = buf[o : o + 32, halves[h]]
                    af[h][r, :] = c * slope[hi, r, halves[h]].astype(F32)
                    if own:
                        sums.add(h, c * sa[hi, r, halves[h]].astype(F32))
            sums.store()

        pipelined(span, 4, lambda rows: dot(grad[rows, :], wp_ref[unit]), hidden)
        tick()
        lax.fori_loop(0, samples // 512, transposed_e, 0)

        for k in range(TAPS):
            put_gw(unit, k, dot(tr[...], cols[own0:own1, k * C : (k + 1) * C]))
        jobs.append(job(4 + 2 * unit))
        jobs.append(job(5 + 2 * unit))
        tick()

        span = (own_rows, near)[unit]
        for k in range(TAPS):
            wt[k * C : (k + 1) * C, :] = wd_ref[unit, :, (TAPS - 1 - k) * C : (TAPS - k) * C]
        shift_pass(unit, span)

        def inner(parts, buf):
            sums = Totals(ui)
            for r, o, own in parts:
                for h in range(2):
                    f = buf[o : o + 32, halves[h]]
                    g = grad[r, halves[h]].astype(F32) + f * slope[ui, r, halves[h]].astype(F32)
                    if unit == 0:
                        g = jnp.where(rem[0, r, :] > 0, g, 0.0)
                    grad[r, halves[h]] = g.astype(BF16)
                    if own:
                        sums.add(h, f * sa[ui, r, halves[h]].astype(F32))
            sums.store()

        pipelined(span, 4, lambda rows: dot(cols[rows, :], wt[...]), inner, mid=True)
        tick()

    backward(1)
    backward(0)

    ga[...] = jnp.zeros_like(ga)
    for i in range(5):
        for h in range(2):
            ga[i : i + 1, halves[h]] = jnp.sum(acc[i, h] * kcol[1, i, h], axis=0, keepdims=True)
    jobs.append(alpha_job())
    tick()

    def sg_body(j, _):
        lanes = pl.ds(pl.multiple_of(j * 512, 128), 512)
        sg_ref[:, lanes] = grad[pl.ds(pl.multiple_of(j * 512 + own0, 16), 512), :].T
        return 0

    lax.fori_loop(0, samples // 512, sg_body, 0)
    while jobs:
        tick()
    links.drain()


def block_and_sums(lengths, sig, og, conv_dilated, conv_point, conv_down, snake_alpha):
    samples = sig.shape[1]
    rows = samples + 2 * LEAD
    rows_j = samples // STRIDE
    vmem = pl.BlockSpec(memory_space=pltpu.VMEM)
    anywhere = pl.BlockSpec(memory_space=pl.ANY)
    dma = pltpu.SemaphoreType.DMA
    n_jobs = len(ORDERS)

    def landing(count):
        return sum(3 * (count // RING ** (s + 1)) for s in range(3))

    outs = (
        jax.ShapeDtypeStruct((2 * C, rows_j), BF16),
        jax.ShapeDtypeStruct((C, samples), BF16),
        jax.ShapeDtypeStruct((8 * JOB_ROWS[0], 128), BF16),
        jax.ShapeDtypeStruct((8 * JOB_ROWS[4], 128), BF16),
        jax.ShapeDtypeStruct((8, C), F32),
    )
    scratch = [
        pltpu.VMEM((rows, TAPS * C), BF16),
        pltpu.VMEM((rows, 128), F32),
        pltpu.VMEM((rows, 128), F32),
        pltpu.VMEM((rows, 128), F32),
        pltpu.VMEM((rows, 128), F32),
        pltpu.VMEM((rows, C), BF16),
        pltpu.VMEM((rows, C), BF16),
        pltpu.VMEM((rows, C), BF16),
        pltpu.VMEM((rows, C), BF16),
        pltpu.VMEM((rows, C), BF16),
        pltpu.VMEM((rows, C), BF16),
        pltpu.VMEM((5, rows, C), BF16),
        pltpu.VMEM((5, rows, C), BF16),
        pltpu.VMEM((C, samples), BF16),
        pltpu.VMEM((2 * STRIDE, rows_j, C), BF16),
        pltpu.VMEM((rows_j + 32, 2 * C), BF16),
        pltpu.VMEM((rows_j + 48, 2 * C), F32),
        pltpu.VMEM((3, rows_j + 16, 2 * C), BF16),
        pltpu.VMEM((TAPS * C, C), BF16),
        pltpu.VMEM((C, C), BF16),
        pltpu.VMEM((2, rows, 128), jnp.int32),
        pltpu.VMEM((2, 5, 2, 8, 128), F32),
        pltpu.VMEM((5, 2, 8, 128), F32),
        pltpu.VMEM((2, 544, C), F32),
        pltpu.VMEM(conv_down.shape, BF16),
        pltpu.VMEM((8 * JOB_ROWS[0], 128), BF16),
        pltpu.VMEM((8 * JOB_ROWS[4], 128), BF16),
        pltpu.VMEM((8, C), F32),
        pltpu.VMEM((4, JOB_ROWS[0], 128), BF16),
        pltpu.VMEM((4, JOB_ROWS[4], 128), BF16),
        pltpu.VMEM((4, landing(JOB_ROWS[0]), 128), BF16),
        pltpu.VMEM((4, landing(JOB_ROWS[4]), 128), BF16),
        pltpu.VMEM((n_jobs, JOB_ROWS[0] // RING**3, 128), BF16),
        pltpu.VMEM((4, RING, 8, C), F32),
        pltpu.VMEM((4, 8, C), F32),
        dma, dma((4,)), dma((4,)), dma((n_jobs,)), dma((n_jobs,)),
        dma((12 * n_jobs,)), dma((12 * n_jobs,)), dma((12 * n_jobs,)), dma((12 * n_jobs,)),
        dma((n_jobs,)), dma((n_jobs, 4)), dma((n_jobs, 4)), dma((4, RING)), dma((4, RING)),
    ]
    return pl.pallas_call(
        functools.partial(block_kernel, samples),
        out_shape=outs,
        in_specs=[pl.BlockSpec(memory_space=pltpu.SMEM)] + [vmem] * 4 + [anywhere, vmem],
        out_specs=(vmem, vmem, anywhere, anywhere, vmem),
        scratch_shapes=scratch,
        compiler_params=pltpu.CompilerParams(
            collective_id=1, has_side_effects=True, vmem_limit_bytes=63 * 1024 * 1024
        ),
        name="encoder_block",
    )(lengths, sig, og, conv_dilated, conv_point, conv_down, snake_alpha)


def widen_kernel(dn_ref, w_ref, out_in, sg_in, ga_in, gdn_ref, gd_ref, gp_ref, out_ref, sg_ref, ga_ref,
                 dn, w, wide_dn, wide_w, in_sem, out_sem, pass_sem):
    passing = [pltpu.make_async_copy(a, b, pass_sem.at[i])
               for i, (a, b) in enumerate(((out_in, out_ref), (sg_in, sg_ref), (ga_in, ga_ref)))]
    steps = 2 * STRIDE
    ins = []
    for i in range(steps):
        d, g = slice(i * 4 * C, (i + 1) * 4 * C), slice(i * 2 * C, (i + 1) * 2 * C)
        ins.append((pltpu.make_async_copy(dn_ref.at[d, :], dn.at[d, :], in_sem.at[0, i]),
                    pltpu.make_async_copy(w_ref.at[g, :], w.at[g, :], in_sem.at[1, i])))
        for copy in ins[-1]:
            copy.start()
    for copy in passing:
        copy.start()
    outs = []
    for i in range(steps):
        unit, k = divmod(i, TAPS + 1)
        for copy in ins[i]:
            copy.wait()
        for h in range(2):
            lanes = slice(h * 128, h * 128 + 128)
            wide_dn[i, :, lanes] = dn[(2 * i + h) * 2 * C : (2 * i + h + 1) * 2 * C, :].astype(F32)
            wide_w[i, :, lanes] = w[(2 * i + h) * C : (2 * i + h + 1) * C, :].astype(F32)
        to = gd_ref.at[unit, :, k * C : (k + 1) * C] if k < TAPS else gp_ref.at[unit]
        outs += [pltpu.make_async_copy(wide_dn.at[i], gdn_ref.at[i], out_sem.at[0, i]),
                 pltpu.make_async_copy(wide_w.at[i], to, out_sem.at[1, i])]
        outs[-2].start()
        outs[-1].start()
    for copy in outs + passing:
        copy.wait()


def widen(fdn, fw, out, sg, ga):
    steps = 2 * STRIDE
    anywhere = pl.BlockSpec(memory_space=pl.ANY)
    dma = pltpu.SemaphoreType.DMA
    return pl.pallas_call(
        widen_kernel,
        out_shape=(
            jax.ShapeDtypeStruct((steps, 2 * C, C), F32),
            jax.ShapeDtypeStruct((2, C, TAPS * C), F32),
            jax.ShapeDtypeStruct((2, C, C), F32),
            jax.ShapeDtypeStruct(out.shape, out.dtype),
            jax.ShapeDtypeStruct(sg.shape, sg.dtype),
            jax.ShapeDtypeStruct(ga.shape, ga.dtype),
        ),
        in_specs=[anywhere] * 5,
        out_specs=(anywhere,) * 6,
        scratch_shapes=[
            pltpu.VMEM(fdn.shape, BF16),
            pltpu.VMEM(fw.shape, BF16),
            pltpu.VMEM((steps, 2 * C, C), F32),
            pltpu.VMEM((steps, C, C), F32),
            dma((2, steps)), dma((2, steps)), dma((3,)),
        ],
        compiler_params=pltpu.CompilerParams(vmem_limit_bytes=63 * 1024 * 1024),
        name="widen",
    )(fdn, fw, out, sg, ga)


def body(signal, lengths, conv_dilated, conv_point, conv_down, snake_alpha, out_grad):
    out, sg, fdn, fw, ga = block_and_sums(
        lengths, signal[0], out_grad[0], conv_dilated, conv_point, conv_down, snake_alpha
    )
    gdn, gd, gp, out, sg, ga = widen(fdn, fw, out, sg, ga)
    return (out[None], sg[None], gd, gp, gdn, ga[:5])


def solution(mesh):
    placed = (P("dp", None, "tm"), P("dp", None), P(), P(), P(), P(), P("dp", None, "tm"))
    return jax.shard_map(
        body,
        mesh=mesh,
        in_specs=placed,
        out_specs=(P("dp", None, "tm"), P("dp", None, "tm"), P(), P(), P(), P()),
        check_vma=False,
    )
```

```python
import functools

import jax
import jax.numpy as jnp
from jax import lax
from jax.experimental import pallas as pl
from jax.experimental.pallas import tpu as pltpu
from jax.sharding import PartitionSpec as P

TAPS = 7
STRIDE = 8
DILATIONS = (3, 9)
TILE = 64
REC = 4
C = 256
LEAD = 112
F32 = jnp.float32
BF16 = jnp.bfloat16

SIN_PI = (3.14158202, -5.16714279, 2.54189898, -0.55463609)
TWO_COS_PI = (1.9999999, -9.86958572, 8.11682382, -2.66376026, 0.43939346)


def dot(a, b):
    return jnp.dot(a, b, preferred_element_type=F32)


def dot_nt(a, b):
    return lax.dot_general(a, b, (((1,), (1,)), ((), ())), preferred_element_type=F32)


def poly(coefs, x):
    total = coefs[-1]
    for c in coefs[-2::-1]:
        total = total * x + c
    return total


def sine_parts(turns):
    f = turns - jnp.round(turns)
    x = f * f
    s = f * poly(SIN_PI, x)
    return s * poly(TWO_COS_PI, x), s * s


RING = 4
MESH = pl.DeviceIdType.MESH
ORDERS = ((0, 1, 2), (1, 2, 0), (2, 0, 1), (1, 2, 0), (2, 0, 1), (0, 1, 2), (2, 1, 0))
N_DOWN = 3
UNIT_OF = (0, 0, 1, 1)
JOB_ROWS = (3072, 3072, 2048) + (1024,) * 4


class Links:
    def __init__(self):
        self.dp, self.tm = lax.axis_index("dp"), lax.axis_index("tm")
        self.core = lax.rem(self.dp, 2)
        self.place = (lax.rem(self.tm, RING), self.dp // 2, self.tm // RING)
        self.sibling = (self.dp + 1 - 2 * self.core, self.tm)
        self.sends = []

    def along(self, axis, step):
        x, y, z = (
            lax.rem(c + step + RING, RING) if a == axis else c for a, c in enumerate(self.place)
        )
        return (y * 2 + self.core, z * RING + x)

    def in_time(self, step):
        count = lax.axis_size("tm")
        return (self.dp, lax.rem(self.tm + step + count, count))

    def peers(self):
        ring = [self.along(a, s) for a in range(3) for s in (1, 2, 3)]
        return [self.sibling, self.in_time(1), self.in_time(-1)] + ring

    def greet(self):
        barrier = pltpu.get_barrier_semaphore()
        for peer in self.peers():
            pl.semaphore_signal(barrier, inc=1, device_id=peer, device_id_type=MESH)

    def met(self):
        pl.semaphore_wait(pltpu.get_barrier_semaphore(), len(self.peers()))

    def remote(self, src, dst, send_sem, recv_sem, dev):
        return pltpu.make_async_remote_copy(
            src_ref=src, dst_ref=dst, send_sem=send_sem, recv_sem=recv_sem,
            device_id=dev, device_id_type=MESH,
        )

    def send(self, *args):
        copy = self.remote(*args)
        copy.start()
        self.sends.append(copy)

    def drain(self):
        for copy in self.sends:
            copy.wait_send()


def block_kernel(samples, len_ref, sig_ref, og_ref, wd_ref, wp_ref, wdn_hbm, al_ref,
                 out_ref, sg_ref, fdn_ref, fw_ref, fa_ref,
                 cols, af0, af1, df0, df1, u0, u1, a0, b0, b1, grad, slope, sa, tr, zcols,
                 gb, gtf, gt, wt, wpt, rem, kcol, acc, hbuf, wdn_ref, gdn, gw, ga,
                 pr, lands, fin, gr, gat,
                 load_sem, halo_s, halo_r, pair_s, pair_r, rs_s, rs_r, ag_s, ag_r, fin_sem, back_s, back_r, ga_s, ga_r):
    load = pltpu.make_async_copy(wdn_hbm, wdn_ref, load_sem)
    load.start()
    links = Links()
    links.greet()
    jobs = []

    def start(job):
        next(job)
        jobs.append(job)

    def tick():
        for job in list(jobs):
            if next(job, True):
                jobs.remove(job)

    u_of, b_of = (u0, u1), (b0, b1)
    af, df = (af0, af1), (df0, df1)
    rows_all = u0.shape[0]
    own0, own1 = LEAD, LEAD + samples
    wide = (own0 - 64, own1 + 64)
    near = (own0 - 32, own1 + 32)
    own_rows = (own0, own1)
    rows_j = samples // STRIDE
    all_j = rows_j + 16
    anchor = lax.axis_index("tm") * samples
    halves = (slice(0, 128), slice(128, 256))

    core = links.core
    place = links.place

    def job_rows(p, hf):
        if p < N_DOWN:
            return gdn, fdn_ref, hf * sum(JOB_ROWS[:N_DOWN]) + sum(JOB_ROWS[:p])
        unit = UNIT_OF[p - N_DOWN]
        before = sum(JOB_ROWS[q] for q in range(N_DOWN, p) if UNIT_OF[q - N_DOWN] == unit)
        half = sum(JOB_ROWS[q] for q in range(N_DOWN, len(ORDERS)) if UNIT_OF[q - N_DOWN] == unit)
        return gw, fw_ref, unit * 2 * half + hf * half + before

    def at(ref, start, count):
        return ref.at[pl.ds(pl.multiple_of(start, 16), count), :]

    def wrap(c):
        return lax.rem(c + RING, RING)

    def add_rows(dst, d0, terms, count):
        step_rows = next(n for n in (256, 128, 96, 64, 48, 32, 16) if count % n == 0)

        def one(i, _):
            v = None
            for ref, r0 in terms:
                t = ref[pl.ds(pl.multiple_of(r0 + i * step_rows, 16), step_rows), :].astype(F32)
                v = t if v is None else v + t
            dst[pl.ds(pl.multiple_of(d0 + i * step_rows, 16), step_rows), :] = v.astype(dst.dtype)
            return 0

        lax.fori_loop(0, count // step_rows, one, 0)

    def job(p):
        axes = ORDERS[p]
        part = JOB_ROWS[p]
        chunk = part // RING
        src, res, other_row = job_rows(p, 1 - core)
        own_row = job_rows(p, core)[2]
        offset = sum(JOB_ROWS[:p])
        w, land = pr.at[offset : offset + part, :], lands.at[offset : offset + part, :]
        last = fin.at[p, 0 : part // RING**3, :]
        ring_first = p < N_DOWN

        def result(row, count):
            return at(res, own_row + row, count)

        def rs(s, i):
            return rs_s.at[(p * 3 + s) * 4 + i], rs_r.at[(p * 3 + s) * 4 + i]

        def ag(s, i):
            return ag_s.at[(p * 3 + s) * 4 + i], ag_r.at[(p * 3 + s) * 4 + i]

        links.send(at(src, other_row, part), w, pair_s.at[p], pair_r.at[p], links.sibling)
        yield False
        links.remote(w, w, pair_s.at[p], pair_r.at[p], links.sibling).wait_recv()
        add_rows(w, 0, ((w, 0), (src, own_row)), part)
        base, bases, free = 0, [], 0
        for s in range(3):
            q = part // RING ** (s + 1)
            h = q // 2
            me = place[axes[s]]
            bases.append(base)
            here = base + me * q
            if s == 0 and ring_first:
                for d, sign in enumerate((1, -1)):
                    links.send(at(w, base + wrap(me + 2) * q + d * h, h), land.at[free + d * h : free + d * h + h, :],
                               *rs(s, d), links.along(axes[s], sign))
                yield False
                for d, sign in enumerate((1, -1)):
                    to = links.along(axes[s], sign)
                    row = base + wrap(me + sign) * q
                    half = land.at[free + d * h : free + d * h + h, :]
                    links.remote(half, half, *rs(s, d), to).wait_recv()
                    add_rows(w, row + d * h, ((w, row + d * h), (land, free + d * h)), h)
                    whole = land.at[free + (d + 1) * q : free + (d + 2) * q, :]
                    links.send(at(w, row, q), whole, *rs(s, 2 + d), to)
                yield False
                for d, sign in enumerate((1, -1)):
                    whole = land.at[free + (d + 1) * q : free + (d + 2) * q, :]
                    links.remote(whole, whole, *rs(s, 2 + d), links.along(axes[s], sign)).wait_recv()
                terms = ((w, here), (land, free + q), (land, free + 2 * q))
            else:
                for k in (2, 1, 3):
                    links.send(at(w, base + wrap(me + k) * q, q), land.at[free + (k - 1) * q : free + k * q, :],
                               *rs(s, k), links.along(axes[s], k))
                yield False
                for k in (1, 3, 2):
                    whole = land.at[free + (k - 1) * q : free + k * q, :]
                    links.remote(whole, whole, *rs(s, k), links.along(axes[s], k)).wait_recv()
                terms = ((w, here),) + tuple((land, free + i * q) for i in range(3))
            if s < 2:
                add_rows(w, here, terms, q)
            else:
                add_rows(last, 0, terms, q)
            base = here
            free += 3 * q
        keep_fin = pltpu.make_async_copy(last, result(base, q), fin_sem.at[p])
        keep_fin.start()
        for s in (2, 1, 0):
            q = part // RING ** (s + 1)
            h = q // 2
            me = place[axes[s]]
            block = result(bases[s] + me * q, q)
            if s == 0 and not ring_first:
                links.send(block, block, back_s.at[p, 0], back_r.at[p, 0], links.sibling)
            if s == 0 and ring_first:
                for d, sign in enumerate((1, -1)):
                    links.send(block, block, *ag(s, d), links.along(axes[s], sign))
                yield False
                for d, sign in enumerate((1, -1)):
                    to = links.along(axes[s], sign)
                    row = bases[s] + wrap(me - sign) * q
                    block = result(row, q)
                    links.remote(block, block, *ag(s, d), to).wait_recv()
                    piece = result(row + d * h, h)
                    links.send(piece, piece, *ag(s, 2 + d), to)
                yield False
                row = bases[s] + wrap(me + 2) * q
                for d, sign in enumerate((1, -1)):
                    piece = result(row + d * h, h)
                    links.remote(piece, piece, *ag(s, 2 + d), links.along(axes[s], sign)).wait_recv()
                block = result(0, part)
                links.send(block, block, back_s.at[p, 0], back_r.at[p, 0], links.sibling)
            else:
                for k in (2, 1, 3):
                    links.send(last if s == 2 else block, block, *ag(s, k), links.along(axes[s], k))
                yield False
                for i, k in enumerate((1, 3, 2)):
                    block = result(bases[s] + wrap(me - k) * q, q)
                    links.remote(block, block, *ag(s, k), links.along(axes[s], k)).wait_recv()
                    if s == 0:
                        links.send(block, block, back_s.at[p, 1 + i], back_r.at[p, 1 + i], links.sibling)
            if s == 2:
                keep_fin.wait()
        yield False
        if ring_first:
            block = at(res, other_row, part)
            links.remote(block, block, back_s.at[p, 0], back_r.at[p, 0], links.sibling).wait_recv()
        else:
            for i, off in enumerate((0, -1, 1, 2)):
                block = at(res, other_row + wrap(place[axes[0]] + off) * chunk, chunk)
                links.remote(block, block, back_s.at[p, i], back_r.at[p, i], links.sibling).wait_recv()
        yield True

    def alpha_job():
        links.send(ga, gr.at[3, 0], ga_s.at[3, 0], ga_r.at[3, 0], links.sibling)
        yield False
        links.remote(ga, gr.at[3, 0], ga_s.at[3, 0], ga_r.at[3, 0], links.sibling).wait_recv()
        gat[0] = ga[...] + gr[3, 0]
        for s in range(3):
            me = place[s]
            gr[s, me] = gat[s]
            for k in range(1, RING):
                links.send(gat.at[s], gr.at[s, me], ga_s.at[s, k], ga_r.at[s, k], links.along(s, k))
            yield False
            for k in range(1, RING):
                links.remote(gat.at[s], gr.at[s, wrap(me - k)], ga_s.at[s, k], ga_r.at[s, k],
                             links.along(s, k)).wait_recv()
            gat[s + 1] = (gr[s, 0] + gr[s, 1]) + (gr[s, 2] + gr[s, 3])
        fa_ref[...] = gat[3]
        yield True

    ends = []
    total = 0
    for r in range(REC):
        total = total + len_ref[0, r]
        ends.append(total * TILE)

    def rem_body(i, _):
        rows = pl.ds(pl.multiple_of(i * 32, 32), 32)
        p = lax.broadcasted_iota(jnp.int32, (32, 128), 0) + (i * 32 - LEAD + anchor)
        hi, lo = jnp.zeros_like(p), jnp.full_like(p, -1)
        start = 0
        for end in ends:
            inside = (p >= start) & (p < end)
            hi = jnp.where(inside, end - p, hi)
            lo = jnp.where(inside, p - start, lo)
            start = end
        rem[0, rows, :] = hi
        rem[1, rows, :] = lo
        return 0

    lax.fori_loop(0, rows_all // 32, rem_body, 0)

    for i in range(5):
        row = jnp.broadcast_to(al_ref[i : i + 1, :], (8, C))
        for h in range(2):
            kcol[0, i, h] = row[:, halves[h]] * (1.0 / 3.14159265358979)
            kcol[1, i, h] = 1.0 / row[:, halves[h]]
    acc[...] = jnp.zeros_like(acc)

    def four(x):
        return jnp.concatenate([x] * 4, axis=0)

    def activate(v, i, h):
        k0 = four(kcol[0, i, h])
        k1 = four(kcol[1, i, h])
        s2, sq = sine_parts(v * k0)
        q = sq * k1
        return v + q, s2, v * s2 - q

    class Totals:
        def __init__(self, i):
            self.i, self.sums = i, [None, None]

        def add(self, h, x):
            x = (x[0:8] + x[8:16]) + (x[16:24] + x[24:32])
            self.sums[h] = x if self.sums[h] is None else self.sums[h] + x

        def store(self):
            for h in range(2):
                if self.sums[h] is not None:
                    acc[self.i, h] += self.sums[h]

    def pieces(lo, hi):
        return [(slice(r, r + 32), r - lo, own0 <= r and r + 32 <= own1) for r in range(lo, hi, 32)]

    def row_loop(lo, hi, fn, group=4):
        cuts = sorted({lo, max(lo, own0), min(hi, own1), hi})
        for a, b in zip(cuts, cuts[1:]):
            own = a >= own0 and b <= own1
            many = group if ((b - a) // 32) % group == 0 else 1

            def step(i, _, own=own, a=a, many=many):
                for n in range(many):
                    fn(pl.ds(pl.multiple_of((i * many + n) * 32 + a, 16), 32), own)
                return 0

            lax.fori_loop(0, (b - a) // (32 * many), step, 0)

    def pipelined(span, blocks, product, use):
        lo, hi = span
        count = (hi - lo) // 32
        starts = [lo + 32 * (count * n // blocks) for n in range(blocks + 1)]
        spans = list(zip(starts, starts[1:]))

        def make(n):
            a, b = spans[n]
            hbuf[n % 2, 0 : b - a, :] = product(slice(a, b))

        make(0)
        for n, (a, b) in enumerate(spans):
            if n + 1 < blocks:
                make(n + 1)
            use(pieces(a, b), hbuf.at[n % 2])

    def forward_weights(unit):
        for k in range(TAPS):
            wt[k * C : (k + 1) * C, :] = wd_ref[unit, :, k * C : (k + 1) * C].T
        wpt[...] = wp_ref[unit].T

    def sig_body(j, _):
        src = pl.ds(pl.multiple_of(j * 512, 128), 512)
        u0[pl.ds(pl.multiple_of(j * 512 + own0, 16), 512), :] = sig_ref[:, src].T
        return 0

    lax.fori_loop(0, samples // 512, sig_body, 0)
    for o in range(2):
        gb[16 : 16 + rows_j, o * C : (o + 1) * C] = og_ref[o * C : (o + 1) * C, :].T

    for h in range(2):
        af[h][...] = jnp.zeros_like(af[h])
        df[h][...] = jnp.zeros_like(df[h])
    forward_weights(0)

    def keep(i, rows, h, s2, t):
        slope[i, rows, halves[h]] = (1.0 + s2).astype(BF16)
        sa[i, rows, halves[h]] = t.astype(BF16)

    def first(rows, own):
        alive = rem[0, rows, :] > 0
        for h in range(2):
            v = jnp.where(alive, u0[rows, halves[h]].astype(F32), 0.0)
            u0[rows, halves[h]] = v.astype(BF16)
            a, s2, t = activate(v, 0, h)
            af[h][rows, :] = a
            a0[rows, halves[h]] = a.astype(BF16)
            keep(0, rows, h, s2, t)

    row_loop(*own_rows, first)

    def shift_pass(unit, span, src=af):
        d = DILATIONS[unit]
        lo, hi = span

        def step(i, _):
            start = i * 32 + lo
            rows = pl.ds(pl.multiple_of(start, 16), 32)
            after, before = rem[0, rows, :], rem[1, rows, :]
            for k in range(TAPS):
                by = (k - TAPS // 2) * d
                for h in range(2):
                    x = src[h][pl.ds(start + by, 32), :]
                    if by > 0:
                        x = jnp.where(after > by, x, 0.0)
                    elif by < 0:
                        x = jnp.where(before >= -by, x, 0.0)
                    cols[rows, k * C + h * 128 : k * C + h * 128 + 128] = x.astype(BF16)
            return 0

        lax.fori_loop(0, (hi - lo) // 32, step, 0)

    def forward(unit, span, blocks, dst):
        b_ref, u_ref = b_of[unit], u_of[unit]
        hi, ui = 2 * unit + 1, 2 * unit + 2
        def hidden(parts, buf):
            for r, o, own in parts:
                for h in range(2):
                    a, s2, t = activate(buf[o : o + 32, halves[h]], hi, h)
                    b_ref[r, halves[h]] = a.astype(BF16)
                    keep(hi, r, h, s2, t)

        pipelined(span, blocks, lambda rows: dot(cols[rows, :], wt[...]), hidden)

        def outer(parts, buf):
            for r, o, own in parts:
                for h in range(2):
                    u = (u_ref[r, halves[h]].astype(F32) + buf[o : o + 32, halves[h]]).astype(BF16)
                    if unit == 0:
                        u1[r, halves[h]] = u
                    a, s2, t = activate(u.astype(F32), ui, h)
                    dst[h][r, :] = a
                    keep(ui, r, h, s2, t)

        pipelined(span, blocks, lambda rows: dot(b_ref[rows, :], wpt[...]), outer)

    inner_rows = (own0 + 64, own1 - 64)
    shift_pass(0, inner_rows)
    forward(0, inner_rows, 4, df)

    links.met()
    halo = []
    for i, (ref, count, lo, hi) in enumerate(((u0, 80, own0, own1), (gb, 16, 16, 16 + rows_j))):
        for side, (step, src, dst) in enumerate(((-1, lo, hi), (1, hi - count, lo - count))):
            n = 2 * i + side
            halo.append(links.remote(ref.at[src : src + count, :], ref.at[dst : dst + count, :],
                                     halo_s.at[n], halo_r.at[n], links.in_time(step)))
    for copy in halo:
        copy.start()
    for copy in halo:
        copy.wait()
    for lo, hi in ((own0 - 96, own0), (own1, own1 + 96)):
        row_loop(lo, hi, first)
    for span in ((wide[0], inner_rows[0]), (inner_rows[1], wide[1])):
        shift_pass(0, span)
        forward(0, span, 1, df)
    forward_weights(1)
    shift_pass(1, wide, df)
    forward(1, wide, 4, af)

    at_j = pl.ds(own0, rows_j, stride=STRIDE)
    after, before = rem[0, at_j, :], rem[1, at_j, :]
    for k in range(2 * STRIDE):
        by = k - STRIDE // 2
        for h in range(2):
            z = af[h][pl.ds(own0 + by, rows_j, stride=STRIDE), :]
            if by < 0:
                z = jnp.where(before >= -by, z, 0.0)
            elif by >= STRIDE:
                z = jnp.where(after > by, z, 0.0)
            zcols[k, :, halves[h]] = z.astype(BF16)

    gtf[8 : 8 + rows_j + 32, :] = gb[...].astype(F32)
    at_m = pl.ds(wide[0], all_j, stride=STRIDE)
    after, before = rem[0, at_m, :], rem[1, at_m, :]
    for o in range(4):
        lanes = slice(o * 128, o * 128 + 128)
        gt[0, :, lanes] = jnp.where(after > 0, gtf[16 : 16 + all_j, lanes], 0.0).astype(BF16)
        gt[1, :, lanes] = jnp.where(before > 0, gtf[15 : 15 + all_j, lanes], 0.0).astype(BF16)
        gt[2, :, lanes] = jnp.where(after > STRIDE, gtf[17 : 17 + all_j, lanes], 0.0).astype(BF16)

    load.wait()

    own = og_ref[...]

    def down_body(k, _):
        d = dot(own, zcols[k]).astype(BF16)
        for h in range(2):
            gdn[pl.ds(pl.multiple_of((2 * k + h) * 2 * C, 16), 2 * C), :] = d[:, halves[h]]
        return 0

    lax.fori_loop(0, 2 * STRIDE, down_body, 0)
    for p in range(N_DOWN):
        start(job(p))

    for o in range(2):
        rows = slice(o * C, (o + 1) * C)
        total = dot_nt(wdn_ref[0, rows, :], zcols[0])
        for k in range(1, 2 * STRIDE):
            total = total + dot_nt(wdn_ref[k, rows, :], zcols[k])
        out_ref[rows, :] = total.astype(BF16)

    for p in range(STRIDE):
        if p < STRIDE // 2:
            d = dot(gt[1], wdn_ref[p + 12])
        else:
            d = dot(gt[2], wdn_ref[p - 4])
        d = d + dot(gt[0], wdn_ref[p + 4])
        for h in range(2):
            df[h][pl.ds(wide[0] + p, all_j, stride=STRIDE), :] = d[:, halves[h]]

    sums = Totals(4)
    for r, _, own_piece in pieces(*wide):
        for h in range(2):
            dz = df[h][r, :]
            grad[r, halves[h]] = (dz * slope[4, r, halves[h]].astype(F32)).astype(BF16)
            if own_piece:
                sums.add(h, dz * sa[4, r, halves[h]].astype(F32))
    sums.store()
    tick()

    def transposed(j, _):
        lanes = pl.ds(pl.multiple_of(j * 512, 128), 512)
        tr[:, lanes] = grad[pl.ds(pl.multiple_of(j * 512 + own0, 16), 512), :].T
        return 0

    def transposed_e(j, _):
        lanes = pl.ds(pl.multiple_of(j * 512, 128), 512)
        rows = pl.ds(pl.multiple_of(j * 512 + own0, 16), 512)
        for h in range(2):
            tr[halves[h], lanes] = af[h][rows, :].astype(BF16).T
        return 0

    def put_gw(unit, k, x):
        for h in range(2):
            first = ((unit * (TAPS + 1) + k) * 2 + h) * C
            gw[first : first + C, :] = x[:, halves[h]].astype(BF16)

    def backward(unit):
        b_ref = b_of[unit]
        hi, ui = 2 * unit + 1, 2 * unit
        span = (near, wide)[unit]
        lax.fori_loop(0, samples // 512, transposed, 0)
        put_gw(unit, TAPS, dot(tr[...], b_ref[own0:own1, :]))
        if unit == 0:

            def again(rows, own):
                for h in range(2):
                    af[h][rows, :] = a0[rows, halves[h]].astype(F32)

            row_loop(*near, again)
            shift_pass(0, own_rows)

        def hidden(parts, buf):
            sums = Totals(hi)
            for r, o, own in parts:
                for h in range(2):
                    c = buf[o : o + 32, halves[h]]
                    af[h][r, :] = c * slope[hi, r, halves[h]].astype(F32)
                    if own:
                        sums.add(h, c * sa[hi, r, halves[h]].astype(F32))
            sums.store()

        pipelined(span, 4, lambda rows: dot(grad[rows, :], wp_ref[unit]), hidden)
        tick()
        lax.fori_loop(0, samples // 512, transposed_e, 0)

        for k in range(TAPS):
            put_gw(unit, k, dot(tr[...], cols[own0:own1, k * C : (k + 1) * C]))
        for p, of in enumerate(UNIT_OF):
            if of == unit:
                start(job(N_DOWN + p))
        if unit == 0:
            tick()

        span = (own_rows, near)[unit]
        for k in range(TAPS):
            wt[k * C : (k + 1) * C, :] = wd_ref[unit, :, (TAPS - 1 - k) * C : (TAPS - k) * C]
        shift_pass(unit, span)

        def inner(parts, buf):
            sums = Totals(ui)
            for r, o, own in parts:
                for h in range(2):
                    f = buf[o : o + 32, halves[h]]
                    g = grad[r, halves[h]].astype(F32) + f * slope[ui, r, halves[h]].astype(F32)
                    if unit == 0:
                        g = jnp.where(rem[0, r, :] > 0, g, 0.0)
                    grad[r, halves[h]] = g.astype(BF16)
                    if own:
                        sums.add(h, f * sa[ui, r, halves[h]].astype(F32))
            sums.store()

        pipelined(span, 4, lambda rows: dot(cols[rows, :], wt[...]), inner)
        tick()

    backward(1)
    backward(0)

    ga[...] = jnp.zeros_like(ga)
    for i in range(5):
        for h in range(2):
            ga[i : i + 1, halves[h]] = jnp.sum(acc[i, h] * kcol[1, i, h], axis=0, keepdims=True)
    start(alpha_job())

    def sg_body(j, _):
        lanes = pl.ds(pl.multiple_of(j * 512, 128), 512)
        sg_ref[:, lanes] = grad[pl.ds(pl.multiple_of(j * 512 + own0, 16), 512), :].T
        return 0

    lax.fori_loop(0, samples // 512, sg_body, 0)
    while jobs:
        tick()
    links.drain()


def block_and_sums(lengths, sig, og, conv_dilated, conv_point, conv_down, snake_alpha):
    samples = sig.shape[1]
    rows = samples + 2 * LEAD
    rows_j = samples // STRIDE
    vmem = pl.BlockSpec(memory_space=pltpu.VMEM)
    anywhere = pl.BlockSpec(memory_space=pl.ANY)
    dma = pltpu.SemaphoreType.DMA
    n_jobs = len(ORDERS)
    outs = (
        jax.ShapeDtypeStruct((2 * C, rows_j), BF16),
        jax.ShapeDtypeStruct((C, samples), BF16),
        jax.ShapeDtypeStruct((2 * sum(JOB_ROWS[:N_DOWN]), 128), BF16),
        jax.ShapeDtypeStruct((2 * sum(JOB_ROWS[N_DOWN:]), 128), BF16),
        jax.ShapeDtypeStruct((8, C), F32),
    )
    scratch = [
        pltpu.VMEM((rows, TAPS * C), BF16),
        pltpu.VMEM((rows, 128), F32),
        pltpu.VMEM((rows, 128), F32),
        pltpu.VMEM((rows, 128), F32),
        pltpu.VMEM((rows, 128), F32),
        pltpu.VMEM((rows, C), BF16),
        pltpu.VMEM((rows, C), BF16),
        pltpu.VMEM((rows, C), BF16),
        pltpu.VMEM((rows, C), BF16),
        pltpu.VMEM((rows, C), BF16),
        pltpu.VMEM((rows, C), BF16),
        pltpu.VMEM((5, rows, C), BF16),
        pltpu.VMEM((5, rows, C), BF16),
        pltpu.VMEM((C, samples), BF16),
        pltpu.VMEM((2 * STRIDE, rows_j, C), BF16),
        pltpu.VMEM((rows_j + 32, 2 * C), BF16),
        pltpu.VMEM((rows_j + 48, 2 * C), F32),
        pltpu.VMEM((3, rows_j + 16, 2 * C), BF16),
        pltpu.VMEM((TAPS * C, C), BF16),
        pltpu.VMEM((C, C), BF16),
        pltpu.VMEM((2, rows, 128), jnp.int32),
        pltpu.VMEM((2, 5, 2, 8, 128), F32),
        pltpu.VMEM((5, 2, 8, 128), F32),
        pltpu.VMEM((2, 544, C), F32),
        pltpu.VMEM(conv_down.shape, BF16),
        pltpu.VMEM((2 * sum(JOB_ROWS[:N_DOWN]), 128), BF16),
        pltpu.VMEM((2 * sum(JOB_ROWS[N_DOWN:]), 128), BF16),
        pltpu.VMEM((8, C), F32),
        pltpu.VMEM((sum(JOB_ROWS), 128), BF16),
        pltpu.VMEM((sum(JOB_ROWS), 128), BF16),
        pltpu.VMEM((n_jobs, JOB_ROWS[0] // RING**3, 128), BF16),
        pltpu.VMEM((4, RING, 8, C), F32),
        pltpu.VMEM((4, 8, C), F32),
        dma, dma((4,)), dma((4,)), dma((n_jobs,)), dma((n_jobs,)),
        dma((12 * n_jobs,)), dma((12 * n_jobs,)), dma((12 * n_jobs,)), dma((12 * n_jobs,)),
        dma((n_jobs,)), dma((n_jobs, 4)), dma((n_jobs, 4)), dma((4, RING)), dma((4, RING)),
    ]
    return pl.pallas_call(
        functools.partial(block_kernel, samples),
        out_shape=outs,
        in_specs=[pl.BlockSpec(memory_space=pltpu.SMEM)] + [vmem] * 4 + [anywhere, vmem],
        out_specs=(vmem, vmem, anywhere, anywhere, vmem),
        scratch_shapes=scratch,
        compiler_params=pltpu.CompilerParams(
            collective_id=1, has_side_effects=True, vmem_limit_bytes=63 * 1024 * 1024
        ),
        name="encoder_block",
    )(lengths, sig, og, conv_dilated, conv_point, conv_down, snake_alpha)


def widen_kernel(dn_ref, w_ref, out_in, sg_in, ga_in, gdn_ref, gd_ref, gp_ref, out_ref, sg_ref, ga_ref,
                 dn, w, wide_dn, wide_w, out_v, sg_v, ga_v, in_sem, out_sem, pass_sem):
    through = ((out_in, out_v, out_ref), (sg_in, sg_v, sg_ref), (ga_in, ga_v, ga_ref))
    passing = [pltpu.make_async_copy(a, v, pass_sem.at[0, i]) for i, (a, v, _) in enumerate(through)]
    steps = 2 * STRIDE
    ins = []
    for i in range(steps):
        d, g = slice(i * 4 * C, (i + 1) * 4 * C), slice(i * 2 * C, (i + 1) * 2 * C)
        ins.append((pltpu.make_async_copy(dn_ref.at[d, :], dn.at[d, :], in_sem.at[0, i]),
                    pltpu.make_async_copy(w_ref.at[g, :], w.at[g, :], in_sem.at[1, i])))
        for copy in ins[-1]:
            copy.start()
    for copy in passing:
        copy.start()
    outs = [pltpu.make_async_copy(v, b, pass_sem.at[1, i]) for i, (_, v, b) in enumerate(through)]
    for i in range(steps):
        unit, k = divmod(i, TAPS + 1)
        for copy in ins[i]:
            copy.wait()
        for h in range(2):
            lanes = slice(h * 128, h * 128 + 128)
            wide_dn[i, :, lanes] = dn[(2 * i + h) * 2 * C : (2 * i + h + 1) * 2 * C, :].astype(F32)
            wide_w[i, :, lanes] = w[(2 * i + h) * C : (2 * i + h + 1) * C, :].astype(F32)
        to = gd_ref.at[unit, :, k * C : (k + 1) * C] if k < TAPS else gp_ref.at[unit]
        outs += [pltpu.make_async_copy(wide_dn.at[i], gdn_ref.at[i], out_sem.at[0, i]),
                 pltpu.make_async_copy(wide_w.at[i], to, out_sem.at[1, i])]
        outs[-2].start()
        outs[-1].start()
        if i == 2:
            for copy, on in zip(passing, outs):
                copy.wait()
                on.start()
    for copy in outs:
        copy.wait()


def widen(fdn, fw, out, sg, ga):
    steps = 2 * STRIDE
    anywhere = pl.BlockSpec(memory_space=pl.ANY)
    dma = pltpu.SemaphoreType.DMA
    return pl.pallas_call(
        widen_kernel,
        out_shape=(
            jax.ShapeDtypeStruct((steps, 2 * C, C), F32),
            jax.ShapeDtypeStruct((2, C, TAPS * C), F32),
            jax.ShapeDtypeStruct((2, C, C), F32),
            jax.ShapeDtypeStruct(out.shape, out.dtype),
            jax.ShapeDtypeStruct(sg.shape, sg.dtype),
            jax.ShapeDtypeStruct(ga.shape, ga.dtype),
        ),
        in_specs=[anywhere] * 5,
        out_specs=(anywhere,) * 6,
        scratch_shapes=[
            pltpu.VMEM(fdn.shape, BF16),
            pltpu.VMEM(fw.shape, BF16),
            pltpu.VMEM((steps, 2 * C, C), F32),
            pltpu.VMEM((steps, C, C), F32),
            pltpu.VMEM(out.shape, out.dtype),
            pltpu.VMEM(sg.shape, sg.dtype),
            pltpu.VMEM(ga.shape, ga.dtype),
            dma((2, steps)), dma((2, steps)), dma((2, 3)),
        ],
        compiler_params=pltpu.CompilerParams(vmem_limit_bytes=63 * 1024 * 1024),
        name="widen",
    )(fdn, fw, out, sg, ga)


def body(signal, lengths, conv_dilated, conv_point, conv_down, snake_alpha, out_grad):
    out, sg, fdn, fw, ga = block_and_sums(
        lengths, signal[0], out_grad[0], conv_dilated, conv_point, conv_down, snake_alpha
    )
    gdn, gd, gp, out, sg, ga = widen(fdn, fw, out, sg, ga)
    return (out[None], sg[None], gd, gp, gdn, ga[:5])


def solution(mesh):
    placed = (P("dp", None, "tm"), P("dp", None), P(), P(), P(), P(), P("dp", None, "tm"))
    return jax.shard_map(
        body,
        mesh=mesh,
        in_specs=placed,
        out_specs=(P("dp", None, "tm"), P("dp", None, "tm"), P(), P(), P(), P()),
        check_vma=False,
    )
```

```python
import functools

import jax
import jax.numpy as jnp
from jax import lax
from jax.experimental import pallas as pl
from jax.experimental.pallas import tpu as pltpu
from jax.sharding import PartitionSpec as P

TAPS = 7
STRIDE = 8
DILATIONS = (3, 9)
TILE = 64
REC = 4
C = 256
LEAD = 112
F32 = jnp.float32
BF16 = jnp.bfloat16

SIN_PI = (3.14158202, -5.16714279, 2.54189898, -0.55463609)
TWO_COS_PI = (1.9999999, -9.86958572, 8.11682382, -2.66376026, 0.43939346)


def dot(a, b):
    return jnp.dot(a, b, preferred_element_type=F32)


def dot_nt(a, b):
    return lax.dot_general(a, b, (((1,), (1,)), ((), ())), preferred_element_type=F32)


def poly(coefs, x):
    total = coefs[-1]
    for c in coefs[-2::-1]:
        total = total * x + c
    return total


def sine_parts(turns):
    f = turns - jnp.round(turns)
    x = f * f
    s = f * poly(SIN_PI, x)
    return s * poly(TWO_COS_PI, x), s * s


RING = 4
MESH = pl.DeviceIdType.MESH
ORDERS = ((0, 1, 2), (1, 2, 0), (2, 0, 1), (1, 2, 0), (2, 0, 1), (0, 1, 2), (2, 1, 0))
N_DOWN = 3
PLANE_JOBS = (3, 4)
JOB_ROWS = (3072, 3072, 2048) + (1024,) * 4


class Links:
    def __init__(self):
        self.dp, self.tm = lax.axis_index("dp"), lax.axis_index("tm")
        self.core = lax.rem(self.dp, 2)
        self.place = (lax.rem(self.tm, RING), self.dp // 2, self.tm // RING)
        self.sibling = (self.dp + 1 - 2 * self.core, self.tm)
        self.sends = []

    def shifted(self, steps):
        x, y, z = (
            lax.rem(c + steps[a] + RING, RING) if a in steps else c for a, c in enumerate(self.place)
        )
        return (y * 2 + self.core, z * RING + x)

    def along(self, axis, step):
        return self.shifted({axis: step})

    def in_time(self, step):
        count = lax.axis_size("tm")
        return (self.dp, lax.rem(self.tm + step + count, count))

    def peers(self):
        ring = [self.along(a, s) for a in range(3) for s in (1, 2, 3)]
        planes = [ORDERS[p][1:] for p in PLANE_JOBS]
        rest = [self.shifted({a: i, b: j}) for a, b in planes for i in (1, 2, 3) for j in (1, 2, 3)]
        return [self.sibling, self.in_time(1), self.in_time(-1)] + ring + rest

    def greet(self):
        barrier = pltpu.get_barrier_semaphore()
        for peer in self.peers():
            pl.semaphore_signal(barrier, inc=1, device_id=peer, device_id_type=MESH)

    def met(self):
        pl.semaphore_wait(pltpu.get_barrier_semaphore(), len(self.peers()))

    def remote(self, src, dst, send_sem, recv_sem, dev):
        return pltpu.make_async_remote_copy(
            src_ref=src, dst_ref=dst, send_sem=send_sem, recv_sem=recv_sem,
            device_id=dev, device_id_type=MESH,
        )

    def send(self, *args):
        copy = self.remote(*args)
        copy.start()
        self.sends.append(copy)

    def drain(self):
        for copy in self.sends:
            copy.wait_send()


def block_kernel(samples, len_ref, sig_ref, og_ref, wd_ref, wp_ref, wdn_hbm, al_ref,
                 out_ref, sg_ref, fdn_ref, fw_ref, fa_ref,
                 cols, af0, af1, df0, df1, u0, u1, a0, b0, b1, grad, slope, sa, tr, zcols,
                 gb, gtf, gt, wt, wpt, rem, kcol, acc, hbuf, wdn_ref, gdn, gw, ga,
                 pr, lands, fin, gr, gat,
                 load_sem, halo_s, halo_r, pair_s, pair_r, rs_s, rs_r, ag_s, ag_r, rsp_s, rsp_r, agp_s, agp_r, fin_sem, back_s, back_r, ga_s, ga_r):
    load = pltpu.make_async_copy(wdn_hbm, wdn_ref, load_sem)
    load.start()
    links = Links()
    links.greet()
    jobs = []

    def start(job):
        next(job)
        jobs.append(job)
        return job

    def tick(which=None):
        for job in list(jobs if which is None else which):
            if next(job, True):
                jobs.remove(job)

    u_of, b_of = (u0, u1), (b0, b1)
    af, df = (af0, af1), (df0, df1)
    rows_all = u0.shape[0]
    own0, own1 = LEAD, LEAD + samples
    wide = (own0 - 64, own1 + 64)
    near = (own0 - 32, own1 + 32)
    own_rows = (own0, own1)
    rows_j = samples // STRIDE
    all_j = rows_j + 16
    anchor = lax.axis_index("tm") * samples
    halves = (slice(0, 128), slice(128, 256))

    core = links.core
    place = links.place

    def job_rows(p, hf):
        if p < N_DOWN:
            return gdn, fdn_ref, 2 * sum(JOB_ROWS[:p]) + hf * JOB_ROWS[p]
        return gw, fw_ref, 2 * sum(JOB_ROWS[N_DOWN:p]) + hf * JOB_ROWS[p]

    def at(ref, start, count):
        return ref.at[pl.ds(pl.multiple_of(start, 16), count), :]

    def wrap(c):
        return lax.rem(c + RING, RING)

    def add_rows(dst, d0, terms, count):
        step_rows = next(n for n in (256, 128, 96, 64, 48, 32, 16) if count % n == 0)

        def one(i, _):
            v = None
            for ref, r0 in terms:
                t = ref[pl.ds(pl.multiple_of(r0 + i * step_rows, 16), step_rows), :].astype(F32)
                v = t if v is None else v + t
            dst[pl.ds(pl.multiple_of(d0 + i * step_rows, 16), step_rows), :] = v.astype(dst.dtype)
            return 0

        lax.fori_loop(0, count // step_rows, one, 0)

    def job(p):
        axes = ORDERS[p]
        part = JOB_ROWS[p]
        chunk = part // RING
        src, res, other_row = job_rows(p, 1 - core)
        own_row = job_rows(p, core)[2]
        offset = sum(JOB_ROWS[:p])
        w, land = pr.at[offset : offset + part, :], lands.at[offset : offset + part, :]
        last = fin.at[p, 0 : part // RING**3, :]
        ring_first = p < N_DOWN

        def result(row, count):
            return at(res, own_row + row, count)

        def rs(s, i):
            return rs_s.at[(p * 3 + s) * 4 + i], rs_r.at[(p * 3 + s) * 4 + i]

        def ag(s, i):
            return ag_s.at[(p * 3 + s) * 4 + i], ag_r.at[(p * 3 + s) * 4 + i]

        links.send(at(src, other_row, part), w, pair_s.at[p], pair_r.at[p], links.sibling)
        yield False
        links.remote(w, w, pair_s.at[p], pair_r.at[p], links.sibling).wait_recv()
        add_rows(w, 0, ((w, 0), (src, own_row)), part)
        base, bases, free = 0, [], 0
        direct = p in PLANE_JOBS
        plane = axes[1:]
        small = chunk // RING**2
        offsets = [(i, j) for i in range(RING) for j in range(RING) if i or j]
        offsets.sort(key=lambda o: -(min(o[0], RING - o[0]) + min(o[1], RING - o[1])))
        slots = {o: i for i, o in enumerate(offsets)}

        def in_plane(step):
            return links.shifted(dict(zip(plane, step)))

        def plane_sems(step, sems):
            i = PLANE_JOBS.index(p) * 15 + slots[step]
            return sems[0].at[i], sems[1].at[i]

        def small_row(step):
            return base + (wrap(place[plane[0]] + step[0]) * RING + wrap(place[plane[1]] + step[1])) * small

        for s in range(1 if direct else 3):
            q = part // RING ** (s + 1)
            h = q // 2
            me = place[axes[s]]
            bases.append(base)
            here = base + me * q
            if s == 0 and ring_first:
                for d, sign in enumerate((1, -1)):
                    links.send(at(w, base + wrap(me + 2) * q + d * h, h), land.at[free + d * h : free + d * h + h, :],
                               *rs(s, d), links.along(axes[s], sign))
                yield False
                for d, sign in enumerate((1, -1)):
                    to = links.along(axes[s], sign)
                    row = base + wrap(me + sign) * q
                    half = land.at[free + d * h : free + d * h + h, :]
                    links.remote(half, half, *rs(s, d), to).wait_recv()
                    add_rows(w, row + d * h, ((w, row + d * h), (land, free + d * h)), h)
                    whole = land.at[free + (d + 1) * q : free + (d + 2) * q, :]
                    links.send(at(w, row, q), whole, *rs(s, 2 + d), to)
                yield False
                for d, sign in enumerate((1, -1)):
                    whole = land.at[free + (d + 1) * q : free + (d + 2) * q, :]
                    links.remote(whole, whole, *rs(s, 2 + d), links.along(axes[s], sign)).wait_recv()
                terms = ((w, here), (land, free + q), (land, free + 2 * q))
            else:
                for k in (2, 1, 3):
                    links.send(at(w, base + wrap(me + k) * q, q), land.at[free + (k - 1) * q : free + k * q, :],
                               *rs(s, k), links.along(axes[s], k))
                yield False
                for k in (1, 3, 2):
                    whole = land.at[free + (k - 1) * q : free + k * q, :]
                    links.remote(whole, whole, *rs(s, k), links.along(axes[s], k)).wait_recv()
                terms = ((w, here),) + tuple((land, free + i * q) for i in range(3))
            if s < 2 or direct:
                add_rows(w, here, terms, q)
            else:
                add_rows(last, 0, terms, q)
            base = here
            free += 3 * q
        if direct:
            q = small
            mine = small_row((0, 0))
            for step in offsets:
                links.send(at(w, small_row(step), small), land.at[free + slots[step] * small : free + (slots[step] + 1) * small, :],
                           *plane_sems(step, (rsp_s, rsp_r)), in_plane(step))
            yield False
            for step in offsets[::-1]:
                block = land.at[free + slots[step] * small : free + (slots[step] + 1) * small, :]
                links.remote(block, block, *plane_sems(step, (rsp_s, rsp_r)), in_plane(step)).wait_recv()
            add_rows(last, 0, ((w, mine),) + tuple((land, free + i * small) for i in range(15)), small)
        keep_fin = pltpu.make_async_copy(last, result(mine if direct else base, q), fin_sem.at[p])
        keep_fin.start()
        if direct:
            for step in offsets:
                links.send(last, result(mine, small), *plane_sems(step, (agp_s, agp_r)), in_plane(step))
            yield False
            for step in offsets[::-1]:
                block = result(small_row((-step[0], -step[1])), small)
                links.remote(block, block, *plane_sems(step, (agp_s, agp_r)), in_plane(step)).wait_recv()
            keep_fin.wait()
        for s in (0,) if direct else (2, 1, 0):
            q = part // RING ** (s + 1)
            h = q // 2
            me = place[axes[s]]
            block = result(bases[s] + me * q, q)
            if s == 0 and not ring_first:
                links.send(block, block, back_s.at[p, 0], back_r.at[p, 0], links.sibling)
            if s == 0 and ring_first:
                for d, sign in enumerate((1, -1)):
                    links.send(block, block, *ag(s, d), links.along(axes[s], sign))
                yield False
                for d, sign in enumerate((1, -1)):
                    to = links.along(axes[s], sign)
                    row = bases[s] + wrap(me - sign) * q
                    block = result(row, q)
                    links.remote(block, block, *ag(s, d), to).wait_recv()
                    piece = result(row + d * h, h)
                    links.send(piece, piece, *ag(s, 2 + d), to)
                yield False
                row = bases[s] + wrap(me + 2) * q
                for d, sign in enumerate((1, -1)):
                    piece = result(row + d * h, h)
                    links.remote(piece, piece, *ag(s, 2 + d), links.along(axes[s], sign)).wait_recv()
                block = result(0, part)
                links.send(block, block, back_s.at[p, 0], back_r.at[p, 0], links.sibling)
            else:
                for k in (2, 1, 3):
                    links.send(last if s == 2 else block, block, *ag(s, k), links.along(axes[s], k))
                yield False
                for i, k in enumerate((1, 3, 2)):
                    block = result(bases[s] + wrap(me - k) * q, q)
                    links.remote(block, block, *ag(s, k), links.along(axes[s], k)).wait_recv()
                    if s == 0:
                        links.send(block, block, back_s.at[p, 1 + i], back_r.at[p, 1 + i], links.sibling)
            if s == 2:
                keep_fin.wait()
        yield False
        if ring_first:
            block = at(res, other_row, part)
            links.remote(block, block, back_s.at[p, 0], back_r.at[p, 0], links.sibling).wait_recv()
        else:
            for i, off in enumerate((0, -1, 1, 2)):
                block = at(res, other_row + wrap(place[axes[0]] + off) * chunk, chunk)
                links.remote(block, block, back_s.at[p, i], back_r.at[p, i], links.sibling).wait_recv()
        yield True

    def alpha_job():
        links.send(ga, gr.at[3, 0], ga_s.at[3, 0], ga_r.at[3, 0], links.sibling)
        yield False
        links.remote(ga, gr.at[3, 0], ga_s.at[3, 0], ga_r.at[3, 0], links.sibling).wait_recv()
        gat[0] = ga[...] + gr[3, 0]
        for s in range(3):
            me = place[s]
            gr[s, me] = gat[s]
            for k in range(1, RING):
                links.send(gat.at[s], gr.at[s, me], ga_s.at[s, k], ga_r.at[s, k], links.along(s, k))
            yield False
            for k in range(1, RING):
                links.remote(gat.at[s], gr.at[s, wrap(me - k)], ga_s.at[s, k], ga_r.at[s, k],
                             links.along(s, k)).wait_recv()
            gat[s + 1] = (gr[s, 0] + gr[s, 1]) + (gr[s, 2] + gr[s, 3])
        fa_ref[...] = gat[3]
        yield True

    ends = []
    total = 0
    for r in range(REC):
        total = total + len_ref[0, r]
        ends.append(total * TILE)

    def rem_body(i, _):
        for n in range(7):
            first = (i * 7 + n) * 32 - 96 + anchor
            lo_end, hi_end = first + 32, first
            start = 0
            for end in ends:
                inside = (first >= start) & (first < end)
                lo_end = jnp.where(inside, start, lo_end)
                hi_end = jnp.where(inside, end, hi_end)
                start = end
            p = lax.broadcasted_iota(jnp.int32, (32, 128), 0) + first
            rows = pl.ds(pl.multiple_of((i * 7 + n) * 32 + 16, 16), 32)
            rem[0, rows, :] = hi_end - p
            rem[1, rows, :] = p - lo_end
        return 0

    rem[:, 0:16, :] = jnp.full((2, 16, 128), -1, jnp.int32)
    rem[:, rows_all - 16 : rows_all, :] = jnp.full((2, 16, 128), -1, jnp.int32)
    lax.fori_loop(0, (rows_all - 32) // (7 * 32), rem_body, 0)

    for i in range(5):
        row = jnp.broadcast_to(al_ref[i : i + 1, :], (8, C))
        for h in range(2):
            kcol[0, i, h] = row[:, halves[h]] * (1.0 / 3.14159265358979)
            kcol[1, i, h] = 1.0 / row[:, halves[h]]
    acc[...] = jnp.zeros_like(acc)

    def four(x):
        return jnp.concatenate([x] * 4, axis=0)

    def activate(v, i, h):
        k0 = four(kcol[0, i, h])
        k1 = four(kcol[1, i, h])
        s2, sq = sine_parts(v * k0)
        q = sq * k1
        return v + q, s2, v * s2 - q

    class Totals:
        def __init__(self, i):
            self.i, self.sums = i, [None, None]

        def add(self, h, x):
            x = (x[0:8] + x[8:16]) + (x[16:24] + x[24:32])
            self.sums[h] = x if self.sums[h] is None else self.sums[h] + x

        def store(self):
            for h in range(2):
                if self.sums[h] is not None:
                    acc[self.i, h] += self.sums[h]

    def pieces(lo, hi):
        return [(slice(r, r + 32), r - lo, own0 <= r and r + 32 <= own1) for r in range(lo, hi, 32)]

    def row_loop(lo, hi, fn, group=4):
        cuts = sorted({lo, max(lo, own0), min(hi, own1), hi})
        for a, b in zip(cuts, cuts[1:]):
            own = a >= own0 and b <= own1
            many = group if ((b - a) // 32) % group == 0 else 1

            def step(i, _, own=own, a=a, many=many):
                for n in range(many):
                    fn(pl.ds(pl.multiple_of((i * many + n) * 32 + a, 16), 32), own)
                return 0

            lax.fori_loop(0, (b - a) // (32 * many), step, 0)

    def pipelined(span, blocks, product, use, mid=None):
        lo, hi = span
        count = (hi - lo) // 32
        starts = [lo + 32 * (count * n // blocks) for n in range(blocks + 1)]
        spans = list(zip(starts, starts[1:]))

        def make(n):
            a, b = spans[n]
            hbuf[n % 2, 0 : b - a, :] = product(slice(a, b))

        make(0)
        for n, (a, b) in enumerate(spans):
            if n + 1 < blocks:
                make(n + 1)
            use(pieces(a, b), hbuf.at[n % 2])
            if n == 1 and mid is not None:
                mid()

    def forward_weights(unit):
        for k in range(TAPS):
            wt[k * C : (k + 1) * C, :] = wd_ref[unit, :, k * C : (k + 1) * C].T
        wpt[...] = wp_ref[unit].T

    def sig_body(j, _):
        src = pl.ds(pl.multiple_of(j * 512, 128), 512)
        u0[pl.ds(pl.multiple_of(j * 512 + own0, 16), 512), :] = sig_ref[:, src].T
        return 0

    lax.fori_loop(0, samples // 512, sig_body, 0)
    for o in range(2):
        gb[16 : 16 + rows_j, o * C : (o + 1) * C] = og_ref[o * C : (o + 1) * C, :].T

    for h in range(2):
        af[h][...] = jnp.zeros_like(af[h])
        df[h][...] = jnp.zeros_like(df[h])
    forward_weights(0)

    def keep(i, rows, h, s2, t):
        slope[i, rows, halves[h]] = (1.0 + s2).astype(BF16)
        sa[i, rows, halves[h]] = t.astype(BF16)

    def first(rows, own):
        alive = rem[0, rows, :] > 0
        for h in range(2):
            v = jnp.where(alive, u0[rows, halves[h]].astype(F32), 0.0)
            u0[rows, halves[h]] = v.astype(BF16)
            a, s2, t = activate(v, 0, h)
            af[h][rows, :] = a
            a0[rows, halves[h]] = a.astype(BF16)
            keep(0, rows, h, s2, t)

    row_loop(*own_rows, first)

    def shift_pass(unit, span, src=af):
        d = DILATIONS[unit]
        lo, hi = span

        def step(i, _):
            start = i * 32 + lo
            rows = pl.ds(pl.multiple_of(start, 16), 32)
            after, before = rem[0, rows, :], rem[1, rows, :]
            for k in range(TAPS):
                by = (k - TAPS // 2) * d
                for h in range(2):
                    x = src[h][pl.ds(start + by, 32), :]
                    if by > 0:
                        x = jnp.where(after > by, x, 0.0)
                    elif by < 0:
                        x = jnp.where(before >= -by, x, 0.0)
                    cols[rows, k * C + h * 128 : k * C + h * 128 + 128] = x.astype(BF16)
            return 0

        lax.fori_loop(0, (hi - lo) // 32, step, 0)

    def forward(unit, span, blocks, dst):
        b_ref, u_ref = b_of[unit], u_of[unit]
        hi, ui = 2 * unit + 1, 2 * unit + 2
        def hidden(parts, buf):
            for r, o, own in parts:
                for h in range(2):
                    a, s2, t = activate(buf[o : o + 32, halves[h]], hi, h)
                    b_ref[r, halves[h]] = a.astype(BF16)
                    keep(hi, r, h, s2, t)

        pipelined(span, blocks, lambda rows: dot(cols[rows, :], wt[...]), hidden)

        def outer(parts, buf):
            for r, o, own in parts:
                for h in range(2):
                    u = (u_ref[r, halves[h]].astype(F32) + buf[o : o + 32, halves[h]]).astype(BF16)
                    if unit == 0:
                        u1[r, halves[h]] = u
                    a, s2, t = activate(u.astype(F32), ui, h)
                    dst[h][r, :] = a
                    keep(ui, r, h, s2, t)

        pipelined(span, blocks, lambda rows: dot(b_ref[rows, :], wpt[...]), outer)

    inner_rows = (own0 + 64, own1 - 64)
    shift_pass(0, inner_rows)
    forward(0, inner_rows, 4, df)

    links.met()
    halo = []
    for i, (ref, count, lo, hi) in enumerate(((u0, 80, own0, own1), (gb, 16, 16, 16 + rows_j))):
        for side, (step, src, dst) in enumerate(((-1, lo, hi), (1, hi - count, lo - count))):
            n = 2 * i + side
            halo.append(links.remote(ref.at[src : src + count, :], ref.at[dst : dst + count, :],
                                     halo_s.at[n], halo_r.at[n], links.in_time(step)))
    for copy in halo:
        copy.start()
    for copy in halo:
        copy.wait()
    for lo, hi in ((own0 - 96, own0), (own1, own1 + 96)):
        row_loop(lo, hi, first)
    for span in ((wide[0], inner_rows[0]), (inner_rows[1], wide[1])):
        shift_pass(0, span)
        forward(0, span, 1, df)
    forward_weights(1)
    shift_pass(1, wide, df)
    forward(1, wide, 4, af)

    at_j = pl.ds(own0, rows_j, stride=STRIDE)
    after, before = rem[0, at_j, :], rem[1, at_j, :]
    for k in range(2 * STRIDE):
        by = k - STRIDE // 2
        for h in range(2):
            z = af[h][pl.ds(own0 + by, rows_j, stride=STRIDE), :]
            if by < 0:
                z = jnp.where(before >= -by, z, 0.0)
            elif by >= STRIDE:
                z = jnp.where(after > by, z, 0.0)
            zcols[k, :, halves[h]] = z.astype(BF16)
        d = dot(og_ref[...], zcols[k]).astype(BF16)
        for h in range(2):
            gdn[(2 * k + h) * 2 * C : (2 * k + h + 1) * 2 * C, :] = d[:, halves[h]]
        for p in range(N_DOWN):
            if 2 * sum(JOB_ROWS[: p + 1]) == (k + 1) * 4 * C:
                start(job(p))


    gtf[8 : 8 + rows_j + 32, :] = gb[...].astype(F32)
    at_m = pl.ds(wide[0], all_j, stride=STRIDE)
    after, before = rem[0, at_m, :], rem[1, at_m, :]
    for o in range(4):
        lanes = slice(o * 128, o * 128 + 128)
        gt[0, :, lanes] = jnp.where(after > 0, gtf[16 : 16 + all_j, lanes], 0.0).astype(BF16)
        gt[1, :, lanes] = jnp.where(before > 0, gtf[15 : 15 + all_j, lanes], 0.0).astype(BF16)
        gt[2, :, lanes] = jnp.where(after > STRIDE, gtf[17 : 17 + all_j, lanes], 0.0).astype(BF16)

    load.wait()
    for p in range(STRIDE):
        if p < STRIDE // 2:
            d = dot(gt[1], wdn_ref[p + 12])
        else:
            d = dot(gt[2], wdn_ref[p - 4])
        d = d + dot(gt[0], wdn_ref[p + 4])
        for h in range(2):
            df[h][pl.ds(wide[0] + p, all_j, stride=STRIDE), :] = d[:, halves[h]]

    sums = Totals(4)
    for r, _, own_piece in pieces(*wide):
        for h in range(2):
            dz = df[h][r, :]
            grad[r, halves[h]] = (dz * slope[4, r, halves[h]].astype(F32)).astype(BF16)
            if own_piece:
                sums.add(h, dz * sa[4, r, halves[h]].astype(F32))
    sums.store()
    tick()

    def transposed(j, _):
        lanes = pl.ds(pl.multiple_of(j * 512, 128), 512)
        tr[:, lanes] = grad[pl.ds(pl.multiple_of(j * 512 + own0, 16), 512), :].T
        return 0

    def transposed_e(j, _):
        lanes = pl.ds(pl.multiple_of(j * 512, 128), 512)
        rows = pl.ds(pl.multiple_of(j * 512 + own0, 16), 512)
        for h in range(2):
            tr[halves[h], lanes] = af[h][rows, :].astype(BF16).T
        return 0

    def put_gw(unit, k, x):
        for h in range(2):
            first = ((unit * (TAPS + 1) + k) * 2 + h) * C
            gw[first : first + C, :] = x[:, halves[h]].astype(BF16)

    def backward(unit):
        b_ref = b_of[unit]
        hi, ui = 2 * unit + 1, 2 * unit
        span = (near, wide)[unit]
        lax.fori_loop(0, samples // 512, transposed, 0)
        put_gw(unit, TAPS, dot(tr[...], b_ref[own0:own1, :]))
        if unit == 0:

            def again(rows, own):
                for h in range(2):
                    af[h][rows, :] = a0[rows, halves[h]].astype(F32)

            row_loop(*near, again)
            shift_pass(0, own_rows)

        def hidden(parts, buf):
            sums = Totals(hi)
            for r, o, own in parts:
                for h in range(2):
                    c = buf[o : o + 32, halves[h]]
                    af[h][r, :] = c * slope[hi, r, halves[h]].astype(F32)
                    if own:
                        sums.add(h, c * sa[hi, r, halves[h]].astype(F32))
            sums.store()

        pipelined(span, 4, lambda rows: dot(grad[rows, :], wp_ref[unit]), hidden)
        tick()
        lax.fori_loop(0, samples // 512, transposed_e, 0)

        started = []
        for k in range(TAPS):
            put_gw(unit, k, dot(tr[...], cols[own0:own1, k * C : (k + 1) * C]))
            if k == TAPS // 2:
                started.append(start(job(N_DOWN + 2 * unit)))
        if unit == 0:
            tick([j for j in jobs if j not in started])
        started.append(start(job(N_DOWN + 2 * unit + 1)))

        span = (own_rows, near)[unit]
        for k in range(TAPS):
            wt[k * C : (k + 1) * C, :] = wd_ref[unit, :, (TAPS - 1 - k) * C : (TAPS - k) * C]
        shift_pass(unit, span)

        def inner(parts, buf):
            sums = Totals(ui)
            for r, o, own in parts:
                for h in range(2):
                    f = buf[o : o + 32, halves[h]]
                    g = grad[r, halves[h]].astype(F32) + f * slope[ui, r, halves[h]].astype(F32)
                    if unit == 0:
                        g = jnp.where(rem[0, r, :] > 0, g, 0.0)
                    grad[r, halves[h]] = g.astype(BF16)
                    if own:
                        sums.add(h, f * sa[ui, r, halves[h]].astype(F32))
            sums.store()

        pipelined(span, 4, lambda rows: dot(cols[rows, :], wt[...]), inner, lambda: tick(started) if unit == 0 else None)
        tick()

    backward(1)
    backward(0)

    ga[...] = jnp.zeros_like(ga)
    for i in range(5):
        for h in range(2):
            ga[i : i + 1, halves[h]] = jnp.sum(acc[i, h] * kcol[1, i, h], axis=0, keepdims=True)
    start(alpha_job())

    for o in range(2):
        rows = slice(o * C, (o + 1) * C)
        total = dot_nt(wdn_ref[0, rows, :], zcols[0])
        for k in range(1, 2 * STRIDE):
            total = total + dot_nt(wdn_ref[k, rows, :], zcols[k])
        out_ref[rows, :] = total.astype(BF16)

    def sg_body(j, _):
        lanes = pl.ds(pl.multiple_of(j * 512, 128), 512)
        sg_ref[:, lanes] = grad[pl.ds(pl.multiple_of(j * 512 + own0, 16), 512), :].T
        return 0

    lax.fori_loop(0, samples // 512, sg_body, 0)
    while jobs:
        tick()
    links.drain()


def block_and_sums(lengths, sig, og, conv_dilated, conv_point, conv_down, snake_alpha):
    samples = sig.shape[1]
    rows = samples + 2 * LEAD
    rows_j = samples // STRIDE
    vmem = pl.BlockSpec(memory_space=pltpu.VMEM)
    anywhere = pl.BlockSpec(memory_space=pl.ANY)
    dma = pltpu.SemaphoreType.DMA
    n_jobs = len(ORDERS)
    outs = (
        jax.ShapeDtypeStruct((2 * C, rows_j), BF16),
        jax.ShapeDtypeStruct((C, samples), BF16),
        jax.ShapeDtypeStruct((2 * sum(JOB_ROWS[:N_DOWN]), 128), BF16),
        jax.ShapeDtypeStruct((2 * sum(JOB_ROWS[N_DOWN:]), 128), BF16),
        jax.ShapeDtypeStruct((8, C), F32),
    )
    scratch = [
        pltpu.VMEM((rows, TAPS * C), BF16),
        pltpu.VMEM((rows, 128), F32),
        pltpu.VMEM((rows, 128), F32),
        pltpu.VMEM((rows, 128), F32),
        pltpu.VMEM((rows, 128), F32),
        pltpu.VMEM((rows, C), BF16),
        pltpu.VMEM((rows, C), BF16),
        pltpu.VMEM((rows, C), BF16),
        pltpu.VMEM((rows, C), BF16),
        pltpu.VMEM((rows, C), BF16),
        pltpu.VMEM((rows, C), BF16),
        pltpu.VMEM((5, rows, C), BF16),
        pltpu.VMEM((5, rows, C), BF16),
        pltpu.VMEM((C, samples), BF16),
        pltpu.VMEM((2 * STRIDE, rows_j, C), BF16),
        pltpu.VMEM((rows_j + 32, 2 * C), BF16),
        pltpu.VMEM((rows_j + 48, 2 * C), F32),
        pltpu.VMEM((3, rows_j + 16, 2 * C), BF16),
        pltpu.VMEM((TAPS * C, C), BF16),
        pltpu.VMEM((C, C), BF16),
        pltpu.VMEM((2, rows, 128), jnp.int32),
        pltpu.VMEM((2, 5, 2, 8, 128), F32),
        pltpu.VMEM((5, 2, 8, 128), F32),
        pltpu.VMEM((2, 544, C), F32),
        pltpu.VMEM(conv_down.shape, BF16),
        pltpu.VMEM((2 * sum(JOB_ROWS[:N_DOWN]), 128), BF16),
        pltpu.VMEM((2 * sum(JOB_ROWS[N_DOWN:]), 128), BF16),
        pltpu.VMEM((8, C), F32),
        pltpu.VMEM((sum(JOB_ROWS), 128), BF16),
        pltpu.VMEM((sum(JOB_ROWS), 128), BF16),
        pltpu.VMEM((n_jobs, JOB_ROWS[0] // RING**3, 128), BF16),
        pltpu.VMEM((4, RING, 8, C), F32),
        pltpu.VMEM((4, 8, C), F32),
        dma, dma((4,)), dma((4,)), dma((n_jobs,)), dma((n_jobs,)),
        dma((12 * n_jobs,)), dma((12 * n_jobs,)), dma((12 * n_jobs,)), dma((12 * n_jobs,)),
        dma((30,)), dma((30,)), dma((30,)), dma((30,)),
        dma((n_jobs,)), dma((n_jobs, 4)), dma((n_jobs, 4)), dma((4, RING)), dma((4, RING)),
    ]
    return pl.pallas_call(
        functools.partial(block_kernel, samples),
        out_shape=outs,
        in_specs=[pl.BlockSpec(memory_space=pltpu.SMEM)] + [vmem] * 4 + [anywhere, vmem],
        out_specs=(vmem, vmem, anywhere, anywhere, vmem),
        scratch_shapes=scratch,
        compiler_params=pltpu.CompilerParams(
            collective_id=1, has_side_effects=True, vmem_limit_bytes=63 * 1024 * 1024
        ),
        name="encoder_block",
    )(lengths, sig, og, conv_dilated, conv_point, conv_down, snake_alpha)


def widen_kernel(dn_ref, w_ref, out_in, sg_in, ga_in, gdn_ref, gd_ref, gp_ref, out_ref, sg_ref, ga_ref,
                 dn, w, wide_dn, wide_w, out_v, sg_v, ga_v, in_sem, out_sem, pass_sem):
    through = ((out_in, out_v, out_ref), (sg_in, sg_v, sg_ref), (ga_in, ga_v, ga_ref))
    passing = [pltpu.make_async_copy(a, v, pass_sem.at[0, i]) for i, (a, v, _) in enumerate(through)]
    steps = 2 * STRIDE
    ins = []
    for i in range(steps):
        d, g = slice(i * 4 * C, (i + 1) * 4 * C), slice(i * 2 * C, (i + 1) * 2 * C)
        ins.append((pltpu.make_async_copy(dn_ref.at[d, :], dn.at[d, :], in_sem.at[0, i]),
                    pltpu.make_async_copy(w_ref.at[g, :], w.at[g, :], in_sem.at[1, i])))
        for copy in ins[-1]:
            copy.start()
    for copy in passing:
        copy.start()
    outs = [pltpu.make_async_copy(v, b, pass_sem.at[1, i]) for i, (_, v, b) in enumerate(through)]
    for i in range(steps):
        unit, k = divmod(i, TAPS + 1)
        for copy in ins[i]:
            copy.wait()
        for h in range(2):
            lanes = slice(h * 128, h * 128 + 128)
            wide_dn[i, :, lanes] = dn[(2 * i + h) * 2 * C : (2 * i + h + 1) * 2 * C, :].astype(F32)
            wide_w[i, :, lanes] = w[(2 * i + h) * C : (2 * i + h + 1) * C, :].astype(F32)
        to = gd_ref.at[unit, :, k * C : (k + 1) * C] if k < TAPS else gp_ref.at[unit]
        outs += [pltpu.make_async_copy(wide_dn.at[i], gdn_ref.at[i], out_sem.at[0, i]),
                 pltpu.make_async_copy(wide_w.at[i], to, out_sem.at[1, i])]
        outs[-2].start()
        outs[-1].start()
        if i == 2:
            for copy, on in zip(passing, outs):
                copy.wait()
                on.start()
    for copy in outs:
        copy.wait()


def widen(fdn, fw, out, sg, ga):
    steps = 2 * STRIDE
    anywhere = pl.BlockSpec(memory_space=pl.ANY)
    dma = pltpu.SemaphoreType.DMA
    return pl.pallas_call(
        widen_kernel,
        out_shape=(
            jax.ShapeDtypeStruct((steps, 2 * C, C), F32),
            jax.ShapeDtypeStruct((2, C, TAPS * C), F32),
            jax.ShapeDtypeStruct((2, C, C), F32),
            jax.ShapeDtypeStruct(out.shape, out.dtype),
            jax.ShapeDtypeStruct(sg.shape, sg.dtype),
            jax.ShapeDtypeStruct(ga.shape, ga.dtype),
        ),
        in_specs=[anywhere] * 5,
        out_specs=(anywhere,) * 6,
        scratch_shapes=[
            pltpu.VMEM(fdn.shape, BF16),
            pltpu.VMEM(fw.shape, BF16),
            pltpu.VMEM((steps, 2 * C, C), F32),
            pltpu.VMEM((steps, C, C), F32),
            pltpu.VMEM(out.shape, out.dtype),
            pltpu.VMEM(sg.shape, sg.dtype),
            pltpu.VMEM(ga.shape, ga.dtype),
            dma((2, steps)), dma((2, steps)), dma((2, 3)),
        ],
        compiler_params=pltpu.CompilerParams(vmem_limit_bytes=63 * 1024 * 1024),
        name="widen",
    )(fdn, fw, out, sg, ga)


def body(signal, lengths, conv_dilated, conv_point, conv_down, snake_alpha, out_grad):
    out, sg, fdn, fw, ga = block_and_sums(
        lengths, signal[0], out_grad[0], conv_dilated, conv_point, conv_down, snake_alpha
    )
    gdn, gd, gp, out, sg, ga = widen(fdn, fw, out, sg, ga)
    return (out[None], sg[None], gd, gp, gdn, ga[:5])


def solution(mesh):
    placed = (P("dp", None, "tm"), P("dp", None), P(), P(), P(), P(), P("dp", None, "tm"))
    return jax.shard_map(
        body,
        mesh=mesh,
        in_specs=placed,
        out_specs=(P("dp", None, "tm"), P("dp", None, "tm"), P(), P(), P(), P()),
        check_vma=False,
    )
```
